256 devices in a mesh: src: 16 (over x, z_hi, core), tgt: 16 (over z_lo, y).
Axes of the slice: x: 4, y: 4, z: 8 (z_hi: 2, z_lo: 4; z = z_hi * 4 + z_lo), core: 2. Of those that a mesh axis runs over, the one named last changes fastest.
Arguments:
- weights: float32 [2, 16, 16, 256, 256], P(None, 'src', 'tgt'), may hold values from -0.375 to 0.375
- slowness_terms: float32 [3], replicated, may hold values from 0.05 to 0.25
Outputs:
- final_weights: float32 [2, 16, 16, 256, 256], P(None, 'src', 'tgt')
The draws below stay inside these ranges and needn't reach their ends.
All inputs are finite; a program needn't handle non-finite values.
Results may differ from the reference program's by a relative error of at most 0.0005.
Values sent between devices are 32-bit elements; how exact they have to be, the bound alone decides.
A program may use at most 64 MiB of HBM per device.

```python
import math
import jax
import jax.numpy as jnp
from jax import lax

QCH = 16
QQ = 256
TX0 = 16
TY0 = 16
PAIRS = 256
SRC_GROUPS = 16
TGT_GROUPS = 16
N_SRC = 16
N_TGT = 16


def block_levels(rng, shape, split, least, largest):
    level, own = 1.0, jax.random.fold_in(rng, 6)
    for dim, shards_of in split:
        heights = jnp.exp(jax.random.uniform(jax.random.fold_in(own, dim), (shards_of,), jnp.float32, least / len(split), largest / len(split)))
        level = level * jnp.repeat(heights, shape[dim] // shards_of).reshape([-1 if axis == dim else 1 for axis in range(len(shape))])
    return level


def normal_values(own_key, extent, spread, bound, pieces=(), held_as=jnp.bfloat16):
    array = spread * jax.random.normal(own_key, extent, jnp.float32)
    if pieces:
        array = array * block_levels(own_key, extent, pieces, -0.22, 0.18)
    return jnp.clip(array, -bound, bound).astype(held_as)


def setup_inputs(seed: int = 0) -> dict:
    arg_keys = jax.random.split(jax.random.key(seed), 3)
    return {
        "weights": normal_values(arg_keys[0], (2, SRC_GROUPS, TGT_GROUPS, PAIRS, QQ), 0.0625, 0.375, ((1, 16), (2, 16)), jnp.float32),
        "slowness_terms": jnp.clip(jax.random.uniform(arg_keys[1], (3,), jnp.float32, 0.05, 0.25), 0.05, 0.25),
    }


TWO_PI = 2.0 * math.pi

def cheb_nodes(node_count):
    counter = jnp.arange(node_count, dtype=jnp.float32)
    return 0.5 - 0.5 * jnp.cos((2.0 * counter + 1.0) * (math.pi / (2.0 * node_count)))

def lagrange_table(node_count):
    nodes = cheb_nodes(node_count)
    halves = jnp.arange(2, dtype=jnp.float32)
    samples = (halves[:, None] + nodes[None, :]) * 0.5
    diagonal_mask = jnp.eye(node_count, dtype=jnp.bool_)
    node_gaps = jnp.where(diagonal_mask, 1.0, nodes[:, None] - nodes[None, :])
    ratios = (samples[None, None, :, :] - nodes[None, :, None, None]) / node_gaps[:, :, None, None]
    ratios = jnp.where(diagonal_mask[:, :, None, None], 1.0, ratios)
    return jnp.prod(ratios, axis=1)

def lagrange_weights(node_count):
    return jnp.transpose(lagrange_table(node_count), (1, 2, 0))

def unit_turns(turns):
    fraction = turns - jnp.floor(turns)
    return (jnp.cos(TWO_PI * fraction), jnp.sin(TWO_PI * fraction))

def slowness_at(place_first, place_second, slowness_terms):
    return slowness_terms[0] + slowness_terms[1] * jnp.sin(TWO_PI * place_first) + slowness_terms[2] * jnp.cos(TWO_PI * place_second)

def box_center(index_values, levels_done, base_boxes, source_count):
    width = source_count / 2.0 ** levels_done
    return (index_values.astype(jnp.float32) + 0.5) * width - 0.5 * base_boxes * source_count

def device_bit(stratum, source_index, target_index, source_bits):
    if stratum < source_bits:
        return source_index // 2 ** stratum % 2
    return target_index // 2 ** (stratum - source_bits) % 2

def source_boxes(source_index, target_index, source_bits, levels):
    box_first = jnp.zeros_like(source_index + target_index)
    box_second = jnp.zeros_like(source_index + target_index)
    for stratum in range(levels):
        picked = device_bit(stratum, source_index, target_index, source_bits)
        if stratum % 2 == 0:
            box_first = box_first + picked * 2 ** (stratum // 2)
        else:
            box_second = box_second + picked * 2 ** (stratum // 2)
    return (box_first, box_second)

def source_geometry(stratum, source_index, target_index, source_bits, levels):
    merge_axis = stratum % 2
    boxes = source_boxes(source_index, target_index, source_bits, levels)
    counts = (2 ** ((levels + 1) // 2), 2 ** (levels // 2))
    done = stratum // 2
    other_done = (stratum + merge_axis) // 2
    child_width = 2.0 ** done / counts[merge_axis]
    other_width = 2.0 ** other_done / counts[1 - merge_axis]
    parent = boxes[merge_axis] // 2 ** (done + 1)
    corner = parent.astype(jnp.float32) * (2.0 * child_width)
    other_corner = (boxes[1 - merge_axis] // 2 ** other_done).astype(jnp.float32) * other_width
    return (corner, child_width, other_corner, other_width)

def target_prefix(merge_axis, upto, source_index, target_index, source_bits):
    prefix = jnp.zeros_like(source_index + target_index)
    for stratum in range(merge_axis, upto, 2):
        prefix = prefix * 2 + device_bit(stratum, source_index, target_index, source_bits)
    return prefix

def merge_level(children, merge_axis, geometry, wave_first, wave_second, slowness_terms, table, node_count):
    corner, child_width, other_corner, other_width = geometry
    span_groups = children.shape[1]
    span_first = children.shape[3]
    span_second = children.shape[4]
    points_box = children.shape[5]
    nodes = cheb_nodes(node_count)
    along_rows = jnp.repeat(nodes, node_count)
    along_columns = jnp.tile(nodes, node_count)
    if merge_axis == 0:
        moving, resting = (along_rows, along_columns)
    else:
        moving, resting = (along_columns, along_rows)
    halves = jnp.arange(2, dtype=jnp.float32)[None, :, None]
    corner = jnp.reshape(corner, (-1, 1, 1))
    other_corner = jnp.reshape(other_corner, (-1, 1, 1))
    child_move = corner + child_width * (halves + moving[None, None, :])
    parent_move = corner + 2.0 * child_width * moving[None, None, :]
    rest_place = other_corner + other_width * resting[None, None, :]
    if merge_axis == 0:
        child_first, child_second = (child_move, rest_place)
        parent_first, parent_second = (parent_move, rest_place)
    else:
        child_first, child_second = (rest_place, child_move)
        parent_first, parent_second = (rest_place, parent_move)
    full_shape = (span_groups, span_first, 2, span_second)
    wave_first = jnp.broadcast_to(wave_first, full_shape)
    wave_second = jnp.broadcast_to(wave_second, full_shape)
    radius = jnp.sqrt(wave_first * wave_first + wave_second * wave_second)
    child_slow = slowness_at(child_first, child_second, slowness_terms)
    child_turns = child_first[:, None, None, None] * wave_first[..., None, None] + child_second[:, None, None, None] * wave_second[..., None, None] + child_slow[:, None, None, None] * radius[..., None, None]
    pre_cos, pre_sin = unit_turns(child_turns)
    arranged = jnp.transpose(children, (0, 1, 3, 4, 2, 5))[:, :, :, None]
    part_real = arranged[0] * pre_cos + arranged[1] * pre_sin
    part_imag = arranged[1] * pre_cos - arranged[0] * pre_sin
    stacked = jnp.stack([part_real, part_imag]).reshape(-1, 2, node_count, node_count)
    if merge_axis == 0:
        interpolated = jnp.einsum('rcsb,cst->rtb', stacked, table, precision=lax.Precision.HIGHEST, preferred_element_type=jnp.float32)
    else:
        interpolated = jnp.einsum('rcas,cst->rat', stacked, table, precision=lax.Precision.HIGHEST, preferred_element_type=jnp.float32)
    interpolated = interpolated.reshape(2, span_groups, span_first, 2, span_second, points_box)
    parent_slow = slowness_at(parent_first, parent_second, slowness_terms)[:, 0]
    parent_turns = parent_first[:, 0][:, None, None, None] * wave_first[..., None] + parent_second[:, 0][:, None, None, None] * wave_second[..., None] + parent_slow[:, None, None, None] * radius[..., None]
    post_cos, post_sin = unit_turns(parent_turns)
    out_real = interpolated[0] * post_cos - interpolated[1] * post_sin
    out_imag = interpolated[0] * post_sin + interpolated[1] * post_cos
    return jnp.stack([out_real, out_imag])

def reference_level(current, stratum, source_bits, levels, slowness_terms, table):
    on_source = stratum < source_bits
    bit_index = stratum if on_source else stratum - source_bits
    merge_axis = stratum % 2
    if on_source:
        arranged = jnp.transpose(current, (2, 0, 1, 3, 4))
    else:
        arranged = jnp.transpose(current, (1, 0, 2, 3, 4))
    count_along = arranged.shape[2]
    count_other = arranged.shape[0]
    upper_count = count_along // 2 ** (bit_index + 1)
    lower_count = 2 ** bit_index
    along_index = jnp.arange(count_along, dtype=jnp.int32)
    counts = (2 ** ((levels + 1) // 2), 2 ** (levels // 2))
    done_first = (stratum + 1) // 2
    done_second = stratum // 2
    half_first = TX0 // 2
    half_second = TY0 // 2
    sibling = jnp.arange(2, dtype=jnp.int32)

    def one_slab(packed):
        slab_tiles, other_value = packed
        other_index = jnp.zeros_like(along_index) + other_value
        if on_source:
            source_index, target_index = (along_index, other_index)
        else:
            source_index, target_index = (other_index, along_index)
        retained = device_bit(stratum, source_index, target_index, source_bits)
        geometry = source_geometry(stratum, source_index, target_index, source_bits, levels)
        prefix_first = target_prefix(0, stratum, source_index, target_index, source_bits)
        prefix_second = target_prefix(1, stratum, source_index, target_index, source_bits)
        if merge_axis == 0:
            regrouped = slab_tiles.reshape(2, upper_count, 2, lower_count, 2, half_first, TY0, QQ)
            children = jnp.transpose(regrouped, (0, 1, 4, 3, 2, 5, 6, 7)).reshape(2, count_along, 2, half_first, TY0, QQ)
            base_index = (prefix_first * 2 + retained)[:, None] * half_first + jnp.arange(half_first, dtype=jnp.int32)[None, :]
            fresh_index = 2 * base_index[:, :, None] + sibling[None, None, :]
            wave_first = box_center(fresh_index, done_first + 1, TX0, counts[0]).reshape(count_along, half_first, 2, 1)
            second_index = prefix_second[:, None] * TY0 + jnp.arange(TY0, dtype=jnp.int32)[None, :]
            wave_second = box_center(second_index, done_second, TY0, counts[1]).reshape(count_along, 1, 1, TY0)
        else:
            regrouped = slab_tiles.reshape(2, upper_count, 2, lower_count, TX0, 2, half_second, QQ)
            children = jnp.transpose(regrouped, (0, 1, 5, 3, 2, 4, 6, 7)).reshape(2, count_along, 2, TX0 * half_second, 1, QQ)
            first_index = prefix_first[:, None] * TX0 + jnp.arange(TX0, dtype=jnp.int32)[None, :]
            centers_first = box_center(first_index, done_first, TX0, counts[0])
            wave_first = jnp.broadcast_to(centers_first[:, :, None], (count_along, TX0, half_second)).reshape(count_along, TX0 * half_second, 1, 1)
            base_index = (prefix_second * 2 + retained)[:, None] * half_second + jnp.arange(half_second, dtype=jnp.int32)[None, :]
            fresh_index = 2 * base_index[:, :, None] + sibling[None, None, :]
            centers_second = box_center(fresh_index, done_second + 1, TY0, counts[1])
            wave_second = jnp.broadcast_to(centers_second[:, None, :, :], (count_along, TX0, half_second, 2)).reshape(count_along, TX0 * half_second, 2, 1)
        merged = merge_level(children, merge_axis, geometry, wave_first, wave_second, slowness_terms, table, QCH)
        return merged.reshape(2, count_along, PAIRS, QQ)
    result = lax.map(one_slab, (arranged, jnp.arange(count_other, dtype=jnp.int32)))
    if on_source:
        return jnp.transpose(result, (1, 2, 0, 3, 4))
    return jnp.transpose(result, (1, 0, 2, 3, 4))

def reference(weights, slowness_terms):
    source_bits = N_SRC.bit_length() - 1
    levels = source_bits + N_TGT.bit_length() - 1
    table = lagrange_weights(QCH)
    current = weights.reshape(2, N_SRC, N_TGT, PAIRS, QQ)
    for stratum in range(levels):
        current = reference_level(current, stratum, source_bits, levels, slowness_terms, table)
    return current
```

```python
import math

import jax
import jax.numpy as jnp
import ml_dtypes
import numpy as np
from jax import lax
from jax.experimental import pallas as pl
from jax.experimental.pallas import tpu as pltpu
from jax.sharding import PartitionSpec as P

MESH = pl.DeviceIdType.MESH
NODES = 16
LANES = 128
PERIOD = 2.0 * math.pi


def nodes_np():
    t = np.arange(NODES, dtype=np.float64)
    return 0.5 - 0.5 * np.cos((2.0 * t + 1.0) * math.pi / (2 * NODES))


def merge_matrix(axis):
    z = nodes_np()
    eye = np.eye(NODES)
    blocks = []
    for c in range(2):
        at = (c + z) / 2.0
        lag = np.ones((NODES, NODES))
        for t in range(NODES):
            for m in range(NODES):
                if m != t:
                    lag[:, t] *= (at - z[m]) / (z[t] - z[m])
        if axis == 0:
            full = lag[:, None, :, None] * eye[None, :, None, :]
        else:
            full = eye[:, None, :, None] * lag[None, :, None, :]
        blocks.append(full.reshape(256, 256))
    return np.concatenate(blocks)


def split_matrix(axis):
    full = merge_matrix(axis)
    high = full.astype(np.float32).astype(ml_dtypes.bfloat16)
    low = (full - high.astype(np.float64)).astype(np.float32).astype(ml_dtypes.bfloat16)
    return np.concatenate([high, low, high])


def fit(fn, count):
    u = 0.125 - 0.125 * np.cos((np.arange(400) + 0.5) * math.pi / 400)
    c = np.polynomial.chebyshev.Chebyshev.fit(u, fn(np.sqrt(u)), count - 1, domain=[0, 0.25])
    return [float(v) for v in c.convert(kind=np.polynomial.Polynomial, domain=[-1, 1]).coef]


SIN_FIT = fit(lambda f: np.sin(math.pi * f) / f, 5)
COS_FIT = fit(lambda f: np.cos(math.pi * f), 6)


def horner(u, coef):
    acc = jnp.full_like(u, coef[-1])
    for v in coef[-2::-1]:
        acc = acc * u + v
    return acc


def unit(turns):
    f = turns - jnp.round(turns)
    u = f * f
    s = f * horner(u, SIN_FIT)
    c = horner(u, COS_FIT)
    return 1.0 - 2.0 * s * s, 2.0 * s * c


def own_bits():
    src, tgt = lax.axis_index("src"), lax.axis_index("tgt")
    bits = [lax.rem(src // 2**m, 2) for m in range(4)]
    return bits + [lax.rem(tgt // 2**m, 2) for m in range(4)]


def chip():
    src, tgt = lax.axis_index("src"), lax.axis_index("tgt")
    x, z_hi, core = src // 4, lax.rem(src // 2, 2), lax.rem(src, 2)
    return x, lax.rem(tgt, 4), z_hi * 4 + tgt // 4, core


def device_of(x, y, z, core):
    return (x * 4 + (z // 4) * 2 + core, lax.rem(z, 4) * 4 + y)


def slot_row(x, y, z):
    z_lo = lax.rem(z, 4)
    return (
        lax.rem(x, 2) * 64
        + lax.rem(y, 2) * 32
        + lax.rem(z_lo, 2) * 16
        + (z // 4) * 8
        + (x // 2) * 4
        + (y // 2) * 2
        + z_lo // 2
    )


def group_of(z):
    z_lo = lax.rem(z, 4)
    return lax.rem(z_lo, 2) * 2 + z_lo // 2


def source_row(x, y, z):
    inner = lax.rem(x, 2) * 16 + lax.rem(y, 2) * 8 + (z // 4) * 4 + (x // 2) * 2 + y // 2
    return group_of(z) * 32 + inner


def exchange_kernel(w_ref, r_ref, raw, packed, pair_send, pair_recv, own_sem, ready, send, recv):
    x, y, z, core = chip()
    bar = pltpu.get_barrier_semaphore()

    def signal(sem, x1, y1, z1, core1):
        pl.semaphore_signal(
            sem, inc=1, device_id=device_of(x1, y1, z1, core1), device_id_type=MESH
        )

    signal(bar, x, y, z, 1 - core)
    for dz in range(1, 8):
        signal(bar, x, y, lax.rem(z + dz, 8), core)
    for d in range(1, 16):
        signal(bar, lax.rem(x + d // 4, 4), lax.rem(y + d % 4, 4), z, core)
    mine = pltpu.make_async_copy(
        w_ref.at[:, pl.ds(core * 128, 128), :], raw.at[core], own_sem
    )
    mine.start()
    pl.semaphore_wait(bar, 23)
    for d in range(1, 16):
        signal(ready, lax.rem(x + d // 4, 4), lax.rem(y + d % 4, 4), z, core)
    swap = pltpu.make_async_remote_copy(
        src_ref=w_ref.at[:, pl.ds((1 - core) * 128, 128), :],
        dst_ref=raw.at[core],
        send_sem=pair_send,
        recv_sem=pair_recv,
        device_id=device_of(x, y, z, 1 - core),
        device_id_type=MESH,
    )
    swap.start()
    mine.wait()
    swap.wait()
    for c in range(2):
        for part in range(2):
            for half in range(2):
                packed[pl.ds(c * 4 + part * 2 + half, 128, stride=8), :] = raw[
                    c, part, :, half * LANES : (half + 1) * LANES
                ]
    pl.semaphore_wait(ready, 15)
    group = group_of(z)
    to_row = source_row(x, y, z) * 8

    def send_one(m, carry):
        dz, dx, dy = (m // 32) + 4 * lax.rem(m // 16, 2), lax.rem(m // 4, 4), lax.rem(m, 4)
        x1, y1, z1 = lax.rem(x + dx, 4), lax.rem(y + dy, 4), lax.rem(z + dz, 8)
        pltpu.make_async_remote_copy(
            src_ref=packed.at[pl.ds(slot_row(x1, y1, z1) * 8, 8), :],
            dst_ref=r_ref.at[pl.ds(to_row, 8), :],
            send_sem=send,
            recv_sem=recv.at[group],
            device_id=device_of(x1, y1, z1, core),
            device_id_type=MESH,
        ).start()
        return carry

    lax.fori_loop(1, 128, send_one, 0)
    pltpu.make_async_copy(
        packed.at[pl.ds(slot_row(x, y, z) * 8, 8), :], r_ref.at[pl.ds(to_row, 8), :], recv.at[group]
    ).start()
    for g in range(4):
        block = r_ref.at[pl.ds(g * 256, 256), :]
        pltpu.make_async_copy(block, block, recv.at[g]).wait()
    sent = packed.at[pl.ds(0, 1016), :]
    pltpu.make_async_copy(sent, sent, send).wait()


def exchange(weights):
    return pl.pallas_call(
        exchange_kernel,
        out_shape=jax.ShapeDtypeStruct((1024, LANES), jnp.float32),
        in_specs=[pl.BlockSpec(memory_space=pl.ANY)],
        out_specs=pl.BlockSpec(memory_space=pltpu.VMEM),
        scratch_shapes=[
            pltpu.VMEM((2, 2, 128, 256), jnp.float32),
            pltpu.VMEM((1024, LANES), jnp.float32),
            pltpu.SemaphoreType.DMA,
            pltpu.SemaphoreType.DMA,
            pltpu.SemaphoreType.DMA,
            pltpu.SemaphoreType.REGULAR,
            pltpu.SemaphoreType.DMA,
            pltpu.SemaphoreType.DMA((4,)),
        ],
        compiler_params=pltpu.CompilerParams(collective_id=0, has_side_effects=True),
    )(weights)


PLACE = {0: 5, 2: 4, 4: 3, 1: 2, 3: 1, 5: 0}
PLACE6 = {0: 5, 2: 4, 4: 3, 1: 2, 3: 1, 5: 0}
PLACE7 = {0: 6, 2: 5, 4: 4, 6: 3, 1: 2, 3: 1, 5: 0}


def bit_of(index, place):
    return jnp.bitwise_and(lax.shift_right_logical(index, place), 1)


def full_index(n, row):
    place = PLACE[n]
    if place >= 3:
        high = lax.shift_right_logical(row, place)
        return lax.shift_left(high, place + 1) + jnp.bitwise_and(row, 2**place - 1)
    per = 5 - place
    return lax.shift_left(jnp.bitwise_and(row, 2**per - 1), place + 1) + lax.shift_right_logical(row, per)


def center(own, js):
    total = own.astype(jnp.float32) * 16.0 - 128.0
    width = 16.0
    for j in js:
        width = width / 2.0
        total = total + (j.astype(jnp.float32) if hasattr(j, "astype") else float(j)) * width
    return total + width / 2.0


def target_center(n, jbits, own):
    first = center(own[0], [jbits[m] for m in range(0, n + 1, 2)])
    second = center(own[1], [jbits[m] for m in range(1, n + 1, 2)])
    return first, second, jnp.sqrt(first * first + second * second)


def shifts(point, axis, slow):
    cos, sin = unit(point)
    if axis == 0:
        return slow[0] + slow[1] * sin
    return slow[2] * cos


def level_table(n, rows, jbits, bbits, own, z, slow, store):
    axis = n % 2
    done = n // 2
    width = 2.0**done / 16.0
    corner = 0.0
    for m in range(n + 2, 8, 2):
        corner = corner + bbits[m].astype(jnp.float32) * (2.0 ** (m // 2) / 16.0)
    last = target_center(n - 2, jbits, own) if n >= 2 else None
    for j in range(2):
        jnew = dict(jbits)
        jnew[n] = j
        new = target_center(n, jnew, own)
        if last is None:
            step_k, step_r = -new[axis], -new[2]
        else:
            step_k, step_r = last[axis] - new[axis], last[2] - new[2]
        for half in range(2 if axis == 0 else 1):
            for c in range(2):
                point = corner + width * (c + z[half])
                turns = point * step_k + shifts(point, axis, slow) * step_r
                store(c, j, half, unit(turns))


def merge(n, children, phases, matrix, rows):
    stacked = []
    for j in range(2):
        cols = ([], [])
        for c in range(2):
            for half in range(2):
                cos, sin = phases(c, j, half if n % 2 == 0 else 0)
                re, im = children[c][0][half], children[c][1][half]
                cols[0].append(re * cos - im * sin)
                cols[1].append(re * sin + im * cos)
        stacked += [jnp.concatenate(cols[0], axis=1), jnp.concatenate(cols[1], axis=1)]
    full = jnp.concatenate(stacked, axis=0)
    high = full.astype(jnp.bfloat16)
    low = (full - high.astype(jnp.float32)).astype(jnp.bfloat16)
    out = jnp.dot(
        jnp.concatenate([high, high, low], axis=1), matrix, preferred_element_type=jnp.float32
    )
    return lambda j, part, half: out[
        (2 * j + part) * rows : (2 * j + part + 1) * rows, half * LANES : (half + 1) * LANES
    ]


def levels_kernel(r_ref, slow_ref, even_ref, odd_ref, o_ref, state, mid, tab, tab6, tab7, last):
    d = own_bits()
    own = (
        d[0] * 8 + d[2] * 4 + d[4] * 2 + d[6],
        d[1] * 8 + d[3] * 4 + d[5] * 2 + d[7],
    )
    slow = [slow_ref[0], slow_ref[1], slow_ref[2]]
    mats = (even_ref, odd_ref)

    def nodes(axis, rows):
        out = []
        for half in range(2 if axis == 0 else 1):
            lane = lax.broadcasted_iota(jnp.int32, (rows, LANES), 1)
            t = lax.shift_right_logical(lane, 4) + 8 * half if axis == 0 else jnp.bitwise_and(lane, 15)
            out.append(0.5 - 0.5 * unit((2.0 * t.astype(jnp.float32) + 1.0) / 64.0)[0])
        return out

    z32 = (nodes(0, 32), nodes(1, 32))
    row = lax.broadcasted_iota(jnp.int32, (32, LANES), 0)
    for n in range(6):
        index = full_index(n, row)
        jbits = {m: bit_of(index, PLACE[m]) for m in range(n)}

        def one_key(key, carry, n=n, index=index, jbits=jbits):
            bbits = {m: bit_of(index, PLACE[m]) for m in range(n + 1, 6)}
            bbits[6] = bbits[7] = key

            def store(c, j, half, value):
                tab[n, key, c, j, half, 0] = value[0]
                tab[n, key, c, j, half, 1] = value[1]

            level_table(n, 32, jbits, bbits, own, z32[n % 2], slow, store)
            return carry

        lax.fori_loop(0, 2, one_key, 0)

    row = lax.broadcasted_iota(jnp.int32, (64, LANES), 0)

    def store6(c, j, half, value):
        tab6[c, j, half, 0] = value[0]
        tab6[c, j, half, 1] = value[1]

    level_table(
        6, 64, {m: bit_of(row, PLACE6[m]) for m in range(6)}, {}, own, nodes(0, 64), slow, store6
    )
    row = lax.broadcasted_iota(jnp.int32, (128, LANES), 0)

    def store7(c, j, half, value):
        tab7[c, j, 0] = value[0]
        tab7[c, j, 1] = value[1]

    jbits7 = {m: bit_of(row, PLACE7[m]) for m in range(7)}
    level_table(7, 128, jbits7, {}, own, nodes(1, 128), slow, store7)

    def group(g, carry):
        keys = (g // 2, lax.rem(g, 2))
        for n in range(6):
            place = PLACE[n]
            if place >= 3:
                size, stride = 2**place, 1
                starts = [k * 2 * size for k in range(32 // size)]
            else:
                size, stride = 32 >> place, 2 ** (place + 1)
                starts = list(range(2**place))

            def pick(c, part, half, starts=starts, size=size, stride=stride, place=place, n=n):
                if n == 0:
                    return r_ref[pl.ds(g * 256 + c * 4 + part * 2 + half, 32, stride=8), :]
                return jnp.concatenate(
                    [
                        state[g, part, half, pl.ds(s + c * 2**place, size, stride=stride), :]
                        for s in starts
                    ]
                )

            children = [
                [[pick(c, part, half) for half in range(2)] for part in range(2)] for c in range(2)
            ]
            key = keys[n % 2]
            out = merge(
                n,
                children,
                lambda c, j, half, n=n, key=key: (
                    tab[n, key, c, j, half, 0],
                    tab[n, key, c, j, half, 1],
                ),
                mats[n % 2][...],
                32,
            )
            for j in range(2):
                for part in range(2):
                    for half in range(2):
                        block = out(j, part, half)
                        for k, s in enumerate(starts):
                            state[g, part, half, pl.ds(s + j * 2**place, size, stride=stride), :] = (
                                block[k * size : (k + 1) * size]
                            )
        return carry

    lax.fori_loop(0, 4, group, 0)

    for b7 in range(2):
        children = [
            [[state[2 * c + b7, part, half] for half in range(2)] for part in range(2)]
            for c in range(2)
        ]
        out = merge(
            6,
            children,
            lambda c, j, half: (tab6[c, j, half, 0], tab6[c, j, half, 1]),
            even_ref[...],
            64,
        )
        for j in range(2):
            for part in range(2):
                for half in range(2):
                    block = out(j, part, half)
                    for k in range(8):
                        mid[b7, part, half, pl.ds(k * 16 + j * 8, 8), :] = block[k * 8 : k * 8 + 8]

    children = [
        [[mid[c, part, half] for half in range(2)] for part in range(2)] for c in range(2)
    ]
    out = merge(
        7, children, lambda c, j, half: (tab7[c, j, 0], tab7[c, j, 1]), odd_ref[...], 128
    )
    first = target_center(6, jbits7, own)
    z_first, z_second = nodes(0, 128), nodes(1, 128)[0]
    for j in range(2):
        second = target_center(7, {**jbits7, 7: j}, own)
        tail = z_second * second[1] + shifts(z_second, 1, slow) * second[2]
        for half in range(2):
            point = z_first[half]
            turns = point * first[0] + shifts(point, 0, slow) * first[2] + tail
            cos, sin = unit(turns)
            re, im = out(j, 0, half), out(j, 1, half)
            last[0, half, pl.ds(j, 128, stride=2), :] = re * cos - im * sin
            last[1, half, pl.ds(j, 128, stride=2), :] = re * sin + im * cos
    for part in range(2):
        for half in range(2):
            o_ref[part, :, half * LANES : (half + 1) * LANES] = last[part, half]


def levels(received, slowness_terms):
    vmem = pl.BlockSpec(memory_space=pltpu.VMEM)
    return pl.pallas_call(
        levels_kernel,
        out_shape=jax.ShapeDtypeStruct((2, 256, 256), jnp.float32),
        in_specs=[vmem, pl.BlockSpec(memory_space=pltpu.SMEM), vmem, vmem],
        out_specs=vmem,
        scratch_shapes=[
            pltpu.VMEM((4, 2, 2, 64, LANES), jnp.float32),
            pltpu.VMEM((2, 2, 2, 128, LANES), jnp.float32),
            pltpu.VMEM((6, 2, 2, 2, 2, 2, 32, LANES), jnp.float32),
            pltpu.VMEM((2, 2, 2, 2, 64, LANES), jnp.float32),
            pltpu.VMEM((2, 2, 2, 128, LANES), jnp.float32),
            pltpu.VMEM((2, 2, 256, LANES), jnp.float32),
        ],
        compiler_params=pltpu.CompilerParams(vmem_limit_bytes=32 * 2**20),
    )(received, slowness_terms, jnp.asarray(split_matrix(0)), jnp.asarray(split_matrix(1)))


def local(weights, slowness_terms):
    received = exchange(weights.reshape(2, 256, 256))
    return levels(received, slowness_terms).reshape(weights.shape)


def solution(mesh):
    return jax.shard_map(
        local,
        mesh=mesh,
        in_specs=(P(None, "src", "tgt", None, None), P()),
        out_specs=P(None, "src", "tgt", None, None),
        check_vma=False,
    )
```

```python
import math

import jax
import jax.numpy as jnp
import numpy as np
from jax import lax
from jax.experimental import pallas as pl
from jax.experimental.pallas import tpu as pltpu
from jax.sharding import PartitionSpec as P

MESH = pl.DeviceIdType.MESH
NODES = 16
LANES = 128
PERIOD = 2.0 * math.pi


def nodes_np():
    t = np.arange(NODES, dtype=np.float64)
    return 0.5 - 0.5 * np.cos((2.0 * t + 1.0) * math.pi / (2 * NODES))


def merge_matrix(axis):
    z = nodes_np()
    eye = np.eye(NODES)
    blocks = []
    for c in range(2):
        at = (c + z) / 2.0
        lag = np.ones((NODES, NODES))
        for t in range(NODES):
            for m in range(NODES):
                if m != t:
                    lag[:, t] *= (at - z[m]) / (z[t] - z[m])
        if axis == 0:
            full = lag[:, None, :, None] * eye[None, :, None, :]
        else:
            full = eye[:, None, :, None] * lag[None, :, None, :]
        blocks.append(full.reshape(256, 256))
    return np.concatenate(blocks)


def even_matrix():
    return merge_matrix(0).astype(np.float32)


def odd_matrix():
    full = merge_matrix(1)
    block = np.concatenate([full[:LANES, :LANES], full[256 : 256 + LANES, :LANES]])
    return block.astype(np.float32)


def fit(fn, count):
    u = 0.125 - 0.125 * np.cos((np.arange(400) + 0.5) * math.pi / 400)
    c = np.polynomial.chebyshev.Chebyshev.fit(u, fn(np.sqrt(u)), count - 1, domain=[0, 0.25])
    return [float(v) for v in c.convert(kind=np.polynomial.Polynomial, domain=[-1, 1]).coef]


SIN_FIT = fit(lambda f: np.sin(math.pi * f) / f, 5)
COS_FIT = fit(lambda f: np.cos(math.pi * f), 6)


def horner(u, coef):
    acc = jnp.full_like(u, coef[-1])
    for v in coef[-2::-1]:
        acc = acc * u + v
    return acc


def unit(turns):
    f = turns - jnp.round(turns)
    u = f * f
    s = f * horner(u, SIN_FIT)
    c = horner(u, COS_FIT)
    return 1.0 - 2.0 * s * s, 2.0 * s * c


def own_bits():
    src, tgt = lax.axis_index("src"), lax.axis_index("tgt")
    bits = [lax.rem(src // 2**m, 2) for m in range(4)]
    return bits + [lax.rem(tgt // 2**m, 2) for m in range(4)]


def chip():
    src, tgt = lax.axis_index("src"), lax.axis_index("tgt")
    x, z_hi, core = src // 4, lax.rem(src // 2, 2), lax.rem(src, 2)
    return x, lax.rem(tgt, 4), z_hi * 4 + tgt // 4, core


def device_of(x, y, z, core):
    return (x * 4 + (z // 4) * 2 + core, lax.rem(z, 4) * 4 + y)


def slot_row(x, y, z):
    z_lo = lax.rem(z, 4)
    return (
        lax.rem(x, 2) * 64
        + lax.rem(y, 2) * 32
        + lax.rem(z_lo, 2) * 16
        + (z // 4) * 8
        + (x // 2) * 4
        + (y // 2) * 2
        + z_lo // 2
    )


def group_of(z):
    z_lo = lax.rem(z, 4)
    return lax.rem(z_lo, 2) * 2 + z_lo // 2


def source_row(x, y, z):
    inner = lax.rem(x, 2) * 16 + lax.rem(y, 2) * 8 + (z // 4) * 4 + (x // 2) * 2 + y // 2
    return group_of(z) * 32 + inner


PLACE = {0: 5, 2: 4, 4: 3, 1: 2, 3: 1, 5: 0}
PLACE7 = {0: 6, 2: 5, 4: 4, 6: 3, 1: 2, 3: 1, 5: 0}


def bit_of(index, place):
    return jnp.bitwise_and(lax.shift_right_logical(index, place), 1)


def full_index(n, row):
    place = PLACE[n]
    if place >= 3:
        high = lax.shift_right_logical(row, place)
        return lax.shift_left(high, place + 1) + jnp.bitwise_and(row, 2**place - 1)
    per = 5 - place
    return lax.shift_left(jnp.bitwise_and(row, 2**per - 1), place + 1) + lax.shift_right_logical(row, per)


def center(own, js):
    total = own.astype(jnp.float32) * 16.0 - 128.0
    width = 16.0
    for j in js:
        width = width / 2.0
        total = total + (j.astype(jnp.float32) if hasattr(j, "astype") else float(j)) * width
    return total + width / 2.0


def target_center(n, jbits, own):
    first = center(own[0], [jbits[m] for m in range(0, n + 1, 2)])
    second = center(own[1], [jbits[m] for m in range(1, n + 1, 2)])
    return first, second, jnp.sqrt(first * first + second * second)


def shifts(point, axis, slow):
    cos, sin = unit(point)
    if axis == 0:
        return slow[0] + slow[1] * sin
    return slow[2] * cos


def level_table(n, rows, jbits, bbits, own, z, slow, store):
    axis = n % 2
    done = n // 2
    width = 2.0**done / 16.0
    corner = 0.0
    for m in range(n + 2, 8, 2):
        corner = corner + bbits[m].astype(jnp.float32) * (2.0 ** (m // 2) / 16.0)
    last = target_center(n - 2, jbits, own) if n >= 2 else None
    for j in range(2):
        jnew = dict(jbits)
        jnew[n] = j
        new = target_center(n, jnew, own)
        if last is None:
            step_k, step_r = -new[axis], -new[2]
        else:
            step_k, step_r = last[axis] - new[axis], last[2] - new[2]
        for half in range(2 if axis == 0 else 1):
            for c in range(2):
                point = corner + width * (c + z[half])
                turns = point * step_k + shifts(point, axis, slow) * step_r
                store(c, j, half, unit(turns))


def halves_first(n, children, phases):
    out = []
    for j in range(2):
        real, imag = [], []
        for c in range(2):
            pairs = [phases(c, j, half if n % 2 == 0 else 0) for half in range(2)]
            re, im = children[c]
            real.append([re[h] * pairs[h][0] - im[h] * pairs[h][1] for h in range(2)])
            imag.append([re[h] * pairs[h][1] + im[h] * pairs[h][0] for h in range(2)])
        out.append((real, imag))
    return out


def high_low(full):
    high = full.astype(jnp.bfloat16)
    return high, (full - high.astype(jnp.float32)).astype(jnp.bfloat16)


def merge(n, blocks, even_ref, odd_ref):
    turned = [halves_first(n, *block) for block in blocks]
    rows = blocks[0][0][0][0][0].shape[0]
    f32 = jnp.float32
    if n % 2 == 0:
        full = jnp.concatenate(
            [
                jnp.concatenate([t[j][part][c][h] for c in range(2) for h in range(2)], axis=1)
                for t in turned
                for j in range(2)
                for part in range(2)
            ]
        )
        count = full.shape[0]
        high, low = high_low(full)
        both = jnp.dot(
            jnp.concatenate([high, low]), even_ref[0:512, :], preferred_element_type=f32
        )
        rest = jnp.dot(high, even_ref[512:1024, :], preferred_element_type=f32)
        total = both[:count] + (both[count:] + rest)

        def out(block, j, part, half):
            first = (block * 4 + 2 * j + part) * rows
            return total[first : first + rows, half * LANES : (half + 1) * LANES]

        return out
    full = jnp.concatenate(
        [
            jnp.concatenate([t[j][part][c][h] for c in range(2)], axis=1)
            for t in turned
            for j in range(2)
            for part in range(2)
            for h in range(2)
        ]
    )
    count = full.shape[0]
    high, low = high_low(full)
    both = jnp.dot(jnp.concatenate([high, low]), odd_ref[...], preferred_element_type=f32)
    total = both[:count, :LANES] + (both[:count, LANES:] + both[count:, :LANES])

    def out(block, j, part, half):
        first = (block * 8 + 4 * j + 2 * part + half) * rows
        return total[first : first + rows]

    return out


def lane_nodes(axis, rows):
    out = []
    for half in range(2 if axis == 0 else 1):
        lane = lax.broadcasted_iota(jnp.int32, (rows, LANES), 1)
        t = lax.shift_right_logical(lane, 4) + 8 * half if axis == 0 else jnp.bitwise_and(lane, 15)
        out.append(0.5 - 0.5 * unit((2.0 * t.astype(jnp.float32) + 1.0) / 64.0)[0])
    return out


def fill_tables(own, slow, tab, tab6, tab7):
    nodes = (lane_nodes(0, 32), lane_nodes(1, 32))
    row = lax.broadcasted_iota(jnp.int32, (32, LANES), 0)
    for n in range(6):
        index = full_index(n, row)
        jbits = {m: bit_of(index, PLACE[m]) for m in range(n)}

        def one_key(key, carry, n=n, index=index, jbits=jbits):
            bbits = {m: bit_of(index, PLACE[m]) for m in range(n + 1, 6)}
            bbits[6] = bbits[7] = key

            def store(c, j, half, value):
                tab[n, key, c, j, half, 0] = value[0]
                tab[n, key, c, j, half, 1] = value[1]

            level_table(n, 32, jbits, bbits, own, nodes[n % 2], slow, store)
            return carry

        lax.fori_loop(0, 2, one_key, 0)
    row = lax.broadcasted_iota(jnp.int32, (64, LANES), 0)
    jbits = {m: bit_of(row, PLACE[m]) for m in range(6)}

    def store6(c, j, half, value):
        tab6[c, j, half, 0] = value[0]
        tab6[c, j, half, 1] = value[1]

    level_table(6, 64, jbits, {}, own, lane_nodes(0, 64), slow, store6)
    row = lax.broadcasted_iota(jnp.int32, (128, LANES), 0)
    jbits = {m: bit_of(row, PLACE7[m]) for m in range(7)}

    def store7(c, j, half, value):
        tab7[c, j, 0] = value[0]
        tab7[c, j, 1] = value[1]

    level_table(7, 128, jbits, {}, own, lane_nodes(1, 128), slow, store7)


def fill_last(own, slow, last):
    row = lax.broadcasted_iota(jnp.int32, (128, LANES), 0)
    jbits = {m: bit_of(row, PLACE7[m]) for m in range(7)}
    first = target_center(6, jbits, own)
    z_first, z_second = lane_nodes(0, 128), lane_nodes(1, 128)[0]
    for j in range(2):
        second = target_center(7, {**jbits, 7: j}, own)
        tail = z_second * second[1] + shifts(z_second, 1, slow) * second[2]
        for half in range(2):
            point = z_first[half]
            cos, sin = unit(point * first[0] + shifts(point, 0, slow) * first[2] + tail)
            last[j, half, 0] = cos
            last[j, half, 1] = sin


def early_levels(groups, r_ref, state, tab, even_ref, odd_ref):
    for n in range(6):
        place = PLACE[n]
        if place >= 3:
            size, stride = 2**place, 1
            starts = [k * 2 * size for k in range(32 // size)]
        else:
            size, stride = 32 >> place, 2 ** (place + 1)
            starts = list(range(2**place))

        def pick(g, c, part, half, n=n, place=place, size=size, stride=stride, starts=starts):
            if n == 0:
                return r_ref[pl.ds(g * 256 + c * 4 + part * 2 + half, 32, stride=8), :]
            return jnp.concatenate(
                [
                    state[g, part, half, pl.ds(s + c * 2**place, size, stride=stride), :]
                    for s in starts
                ]
            )

        blocks = []
        for g, b6, b7 in groups:
            children = [
                [[pick(g, c, part, half) for half in range(2)] for part in range(2)]
                for c in range(2)
            ]
            key = b7 if n % 2 else b6

            def phases(c, j, half, n=n, key=key):
                return tab[n, key, c, j, half, 0], tab[n, key, c, j, half, 1]

            blocks.append((children, phases))
        out = merge(n, blocks, even_ref, odd_ref)
        for at, (g, _, _) in enumerate(groups):
            for j in range(2):
                for part in range(2):
                    for half in range(2):
                        block = out(at, j, part, half)
                        for k, s in enumerate(starts):
                            state[
                                g, part, half, pl.ds(s + j * 2**place, size, stride=stride), :
                            ] = block[k * size : (k + 1) * size]


def late_levels(state, mid, tab6, tab7, last, fin, even_ref, odd_ref, o_ref):
    blocks = []
    for b7 in range(2):
        children = [
            [[state[2 * c + b7, part, half] for half in range(2)] for part in range(2)]
            for c in range(2)
        ]
        blocks.append((children, lambda c, j, half: (tab6[c, j, half, 0], tab6[c, j, half, 1])))
    out = merge(6, blocks, even_ref, odd_ref)
    for b7 in range(2):
        for j in range(2):
            for part in range(2):
                for half in range(2):
                    block = out(b7, j, part, half)
                    for k in range(8):
                        mid[b7, part, half, pl.ds(k * 16 + j * 8, 8), :] = block[k * 8 : k * 8 + 8]
    children = [
        [[mid[c, part, half] for half in range(2)] for part in range(2)] for c in range(2)
    ]
    block = (children, lambda c, j, half: (tab7[c, j, 0], tab7[c, j, 1]))
    out = merge(7, [block], even_ref, odd_ref)
    for j in range(2):
        for half in range(2):
            cos, sin = last[j, half, 0], last[j, half, 1]
            re, im = out(0, j, 0, half), out(0, j, 1, half)
            fin[0, half, pl.ds(j, 128, stride=2), :] = re * cos - im * sin
            fin[1, half, pl.ds(j, 128, stride=2), :] = re * sin + im * cos
    for part in range(2):
        for half in range(2):
            o_ref[part, :, half * LANES : (half + 1) * LANES] = fin[part, half]


def kernel(
    w_ref, slow_hbm, even_hbm, odd_hbm, o_ref,
    raw, packed, r_ref, even_raw, odd_raw, even_ref, odd_ref, slow_ref, state, mid, tab, tab6, tab7, last, fin,
    pair_send, pair_recv, own_sem, load_sem, ready, send, recv,
):
    x, y, z, core = chip()
    bar = pltpu.get_barrier_semaphore()

    def signal(sem, x1, y1, z1, core1):
        pl.semaphore_signal(
            sem, inc=1, device_id=device_of(x1, y1, z1, core1), device_id_type=MESH
        )

    signal(bar, x, y, z, 1 - core)
    for dz in range(1, 8):
        signal(bar, x, y, lax.rem(z + dz, 8), core)
    for d in range(1, 16):
        signal(bar, lax.rem(x + d // 4, 4), lax.rem(y + d % 4, 4), z, core)
    mine = pltpu.make_async_copy(
        w_ref.at[:, pl.ds(core * 128, 128), :], raw.at[core], own_sem
    )
    mine.start()
    loads = [
        pltpu.make_async_copy(a, b, load_sem.at[k])
        for k, (a, b) in enumerate(
            [(slow_hbm, slow_ref), (even_hbm, even_raw), (odd_hbm, odd_raw)]
        )
    ]
    for load in loads:
        load.start()
    pl.semaphore_wait(bar, 23)
    for d in range(1, 16):
        signal(ready, lax.rem(x + d // 4, 4), lax.rem(y + d % 4, 4), z, core)
    swap = pltpu.make_async_remote_copy(
        src_ref=w_ref.at[:, pl.ds((1 - core) * 128, 128), :],
        dst_ref=raw.at[core],
        send_sem=pair_send,
        recv_sem=pair_recv,
        device_id=device_of(x, y, z, 1 - core),
        device_id_type=MESH,
    )
    swap.start()
    mine.wait()
    swap.wait()
    for c in range(2):
        for part in range(2):
            for half in range(2):
                packed[pl.ds(c * 4 + part * 2 + half, 128, stride=8), :] = raw[
                    c, part, :, half * LANES : (half + 1) * LANES
                ]
    pl.semaphore_wait(ready, 15)
    group = group_of(z)
    to_row = source_row(x, y, z) * 8

    def send_to(dx, dy, dz):
        x1, y1, z1 = lax.rem(x + dx, 4), lax.rem(y + dy, 4), lax.rem(z + dz, 8)
        pltpu.make_async_remote_copy(
            src_ref=packed.at[pl.ds(slot_row(x1, y1, z1) * 8, 8), :],
            dst_ref=r_ref.at[pl.ds(to_row, 8), :],
            send_sem=send,
            recv_sem=recv.at[group],
            device_id=device_of(x1, y1, z1, core),
            device_id_type=MESH,
        ).start()

    def send_a(m, carry):
        send_to(m // 8, lax.rem(m // 2, 4), 4 * lax.rem(m, 2))
        return carry

    def send_b(m, carry):
        send_to(m // 8, lax.rem(m // 2, 4), 2 + 4 * lax.rem(m, 2))
        return carry

    def send_c(m, carry):
        send_to(m // 16, lax.rem(m // 4, 4), 1 + 2 * lax.rem(m, 4))
        return carry

    pltpu.make_async_copy(
        packed.at[pl.ds(slot_row(x, y, z) * 8, 8), :], r_ref.at[pl.ds(to_row, 8), :], recv.at[group]
    ).start()
    lax.fori_loop(1, 32, send_a, 0)
    lax.fori_loop(0, 32, send_b, 0)
    lax.fori_loop(0, 64, send_c, 0)

    for load in loads:
        load.wait()
    even_ref[0:512, :], even_ref[512:1024, :] = high_low(even_raw[...])
    odd_ref[:, 0:LANES], odd_ref[:, LANES : 2 * LANES] = high_low(odd_raw[...])
    d = own_bits()
    own = (
        d[0] * 8 + d[2] * 4 + d[4] * 2 + d[6],
        d[1] * 8 + d[3] * 4 + d[5] * 2 + d[7],
    )
    slow = [slow_ref[0], slow_ref[1], slow_ref[2]]
    fill_tables(own, slow, tab, tab6, tab7)
    fill_last(own, slow, last)

    def arrive(g):
        block = r_ref.at[pl.ds(g * 256, 256), :]
        pltpu.make_async_copy(block, block, recv.at[g]).wait()

    b6, b7 = d[6], d[7]

    def near(k, carry):
        far7 = k + b7 - 2 * k * b7
        g = 2 * b6 + far7
        arrive(g)
        early_levels([(g, b6, far7)], r_ref, state, tab, even_ref, odd_ref)
        return carry

    lax.fori_loop(0, 2, near, 0)
    g = 2 * (1 - b6)
    arrive(g)
    arrive(g + 1)
    early_levels([(g, 1 - b6, 0), (g + 1, 1 - b6, 1)], r_ref, state, tab, even_ref, odd_ref)
    late_levels(state, mid, tab6, tab7, last, fin, even_ref, odd_ref, o_ref)
    sent = packed.at[pl.ds(0, 1016), :]
    pltpu.make_async_copy(sent, sent, send).wait()


def butterfly(weights, slowness_terms):
    hbm = pl.BlockSpec(memory_space=pltpu.HBM)
    f32, bf16 = jnp.float32, jnp.bfloat16
    return pl.pallas_call(
        kernel,
        out_shape=pltpu.VMEM((2, 256, 256), f32),
        in_specs=[hbm] * 4,
        out_specs=pl.BlockSpec(memory_space=pltpu.VMEM),
        scratch_shapes=[
            pltpu.VMEM((2, 2, 128, 256), f32),
            pltpu.VMEM((1024, LANES), f32),
            pltpu.VMEM((1024, LANES), f32),
            pltpu.VMEM((512, 256), f32),
            pltpu.VMEM((256, LANES), f32),
            pltpu.VMEM((1024, 256), bf16),
            pltpu.VMEM((256, 256), bf16),
            pltpu.SMEM((3,), f32),
            pltpu.VMEM((4, 2, 2, 64, LANES), f32),
            pltpu.VMEM((2, 2, 2, 128, LANES), f32),
            pltpu.VMEM((6, 2, 2, 2, 2, 2, 32, LANES), f32),
            pltpu.VMEM((2, 2, 2, 2, 64, LANES), f32),
            pltpu.VMEM((2, 2, 2, 128, LANES), f32),
            pltpu.VMEM((2, 2, 2, 128, LANES), f32),
            pltpu.VMEM((2, 2, 256, LANES), f32),
            pltpu.SemaphoreType.DMA,
            pltpu.SemaphoreType.DMA,
            pltpu.SemaphoreType.DMA,
            pltpu.SemaphoreType.DMA((3,)),
            pltpu.SemaphoreType.REGULAR,
            pltpu.SemaphoreType.DMA,
            pltpu.SemaphoreType.DMA((4,)),
        ],
        compiler_params=pltpu.CompilerParams(
            collective_id=0, has_side_effects=True, vmem_limit_bytes=48 * 2**20
        ),
    )(
        *(
            pltpu.with_memory_space_constraint(a, pltpu.HBM)
            for a in (
                weights,
                slowness_terms,
                jnp.asarray(even_matrix()),
                jnp.asarray(odd_matrix()),
            )
        )
    )


def local(weights, slowness_terms):
    return butterfly(weights.reshape(2, 256, 256), slowness_terms).reshape(weights.shape)


def solution(mesh):
    return jax.shard_map(
        local,
        mesh=mesh,
        in_specs=(P(None, "src", "tgt", None, None), P()),
        out_specs=P(None, "src", "tgt", None, None),
        check_vma=False,
    )
```

```python
import math

import jax
import jax.numpy as jnp
import numpy as np
from jax import lax
from jax.experimental import pallas as pl
from jax.experimental.pallas import tpu as pltpu
from jax.sharding import PartitionSpec as P

MESH = pl.DeviceIdType.MESH
NODES = 16
LANES = 128
PERIOD = 2.0 * math.pi


def nodes_np():
    t = np.arange(NODES, dtype=np.float64)
    return 0.5 - 0.5 * np.cos((2.0 * t + 1.0) * math.pi / (2 * NODES))


def merge_matrix(axis):
    z = nodes_np()
    eye = np.eye(NODES)
    blocks = []
    for c in range(2):
        at = (c + z) / 2.0
        lag = np.ones((NODES, NODES))
        for t in range(NODES):
            for m in range(NODES):
                if m != t:
                    lag[:, t] *= (at - z[m]) / (z[t] - z[m])
        if axis == 0:
            full = lag[:, None, :, None] * eye[None, :, None, :]
        else:
            full = eye[:, None, :, None] * lag[None, :, None, :]
        blocks.append(full.reshape(256, 256))
    return np.concatenate(blocks)


def even_matrix():
    return merge_matrix(0).astype(np.float32)


def odd_matrix():
    full = merge_matrix(1)
    block = np.concatenate([full[:LANES, :LANES], full[256 : 256 + LANES, :LANES]])
    return block.astype(np.float32)


def fit(fn, count):
    u = 0.125 - 0.125 * np.cos((np.arange(400) + 0.5) * math.pi / 400)
    c = np.polynomial.chebyshev.Chebyshev.fit(u, fn(np.sqrt(u)), count - 1, domain=[0, 0.25])
    return [float(v) for v in c.convert(kind=np.polynomial.Polynomial, domain=[-1, 1]).coef]


SIN_FIT = fit(lambda f: np.sin(math.pi * f) / f, 5)
COS_FIT = fit(lambda f: np.cos(math.pi * f), 6)


def horner(u, coef):
    acc = jnp.full_like(u, coef[-1])
    for v in coef[-2::-1]:
        acc = acc * u + v
    return acc


def unit(turns):
    f = turns - jnp.round(turns)
    u = f * f
    s = f * horner(u, SIN_FIT)
    c = horner(u, COS_FIT)
    return 1.0 - 2.0 * s * s, 2.0 * s * c


def own_bits():
    src, tgt = lax.axis_index("src"), lax.axis_index("tgt")
    bits = [lax.rem(src // 2**m, 2) for m in range(4)]
    return bits + [lax.rem(tgt // 2**m, 2) for m in range(4)]


def chip():
    src, tgt = lax.axis_index("src"), lax.axis_index("tgt")
    x, z_hi, core = src // 4, lax.rem(src // 2, 2), lax.rem(src, 2)
    return x, lax.rem(tgt, 4), z_hi * 4 + tgt // 4, core


def along_x(x, step):
    a = lax.rem(x + step, 4)
    return a * 4, lax.rem(a, 2) * 64 + (a // 2) * 4


def along_y(y, step):
    a = lax.rem(y + step, 4)
    return a, lax.rem(a, 2) * 32 + (a // 2) * 2


def along_z(z, step, core):
    a = lax.rem(z + step, 8)
    low, high = lax.rem(a, 4), a // 4
    return high * 2 + core, low * 4, lax.rem(low, 2) * 16 + high * 8 + low // 2


def tile_in_group(d):
    return d[2] * 16 + d[6] * 8 + d[1] * 4 + d[3] * 2 + d[7]


PLACE = {0: 5, 2: 4, 6: 3, 1: 2, 3: 1, 7: 0}


def bit_of(index, place):
    return jnp.bitwise_and(lax.shift_right_logical(index, place), 1)


def full_index(n, row):
    place = PLACE[n]
    if place >= 3:
        high = lax.shift_right_logical(row, place)
        return lax.shift_left(high, place + 1) + jnp.bitwise_and(row, 2**place - 1)
    per = 5 - place
    return lax.shift_left(jnp.bitwise_and(row, 2**per - 1), place + 1) + lax.shift_right_logical(row, per)


def center(own, js):
    total = own.astype(jnp.float32) * 16.0 - 128.0
    width = 16.0
    for j in js:
        width = width / 2.0
        total = total + (j.astype(jnp.float32) if hasattr(j, "astype") else float(j)) * width
    return total + width / 2.0


def target_center(n, jbits, own):
    first = center(own[0], [jbits[m] for m in range(0, n + 1, 2)])
    second = center(own[1], [jbits[m] for m in range(1, n + 1, 2)])
    return first, second, jnp.sqrt(first * first + second * second)


def shifts(point, axis, slow):
    cos, sin = unit(point)
    if axis == 0:
        return slow[0] + slow[1] * sin
    return slow[2] * cos


def level_table(n, rows, jbits, bbits, own, z, slow, store):
    axis = n % 2
    done = n // 2
    width = 2.0**done / 16.0
    corner = 0.0
    for m in range(n + 2, 8, 2):
        corner = corner + bbits[m].astype(jnp.float32) * (2.0 ** (m // 2) / 16.0)
    last = target_center(n - 2, jbits, own) if n >= 2 else None
    for j in range(2):
        jnew = dict(jbits)
        jnew[n] = j
        new = target_center(n, jnew, own)
        if last is None:
            step_k, step_r = -new[axis], -new[2]
        else:
            step_k, step_r = last[axis] - new[axis], last[2] - new[2]
        for half in range(2 if axis == 0 else 1):
            for c in range(2):
                point = corner + width * (c + z[half])
                turns = point * step_k + shifts(point, axis, slow) * step_r
                store(c, j, half, unit(turns))


def halves_first(n, children, phases):
    out = []
    for j in range(2):
        real, imag = [], []
        for c in range(2):
            pairs = [phases(c, j, half if n % 2 == 0 else 0) for half in range(2)]
            re, im = children[c]
            real.append([re[h] * pairs[h][0] - im[h] * pairs[h][1] for h in range(2)])
            imag.append([re[h] * pairs[h][1] + im[h] * pairs[h][0] for h in range(2)])
        out.append((real, imag))
    return out


def high_low(full):
    high = full.astype(jnp.bfloat16)
    return high, (full - high.astype(jnp.float32)).astype(jnp.bfloat16)


def merge(n, blocks, even_ref, odd_ref):
    turned = [halves_first(n, *block) for block in blocks]
    rows = blocks[0][0][0][0][0].shape[0]
    f32 = jnp.float32
    if n % 2 == 0:
        full = jnp.concatenate(
            [
                jnp.concatenate([t[j][part][c][h] for c in range(2) for h in range(2)], axis=1)
                for t in turned
                for j in range(2)
                for part in range(2)
            ]
        )
        count = full.shape[0]
        high, low = high_low(full)
        both = jnp.dot(
            jnp.concatenate([high, low]), even_ref[0:512, :], preferred_element_type=f32
        )
        rest = jnp.dot(high, even_ref[512:1024, :], preferred_element_type=f32)
        total = both[:count] + (both[count:] + rest)

        def out(block, j, part, half):
            first = (block * 4 + 2 * j + part) * rows
            return total[first : first + rows, half * LANES : (half + 1) * LANES]

        return out
    full = jnp.concatenate(
        [
            jnp.concatenate([t[j][part][c][h] for c in range(2)], axis=1)
            for t in turned
            for j in range(2)
            for part in range(2)
            for h in range(2)
        ]
    )
    count = full.shape[0]
    high, low = high_low(full)
    both = jnp.dot(jnp.concatenate([high, low]), odd_ref[...], preferred_element_type=f32)
    total = both[:count, :LANES] + (both[:count, LANES:] + both[count:, :LANES])

    def out(block, j, part, half):
        first = (block * 8 + 4 * j + 2 * part + half) * rows
        return total[first : first + rows]

    return out


def lane_nodes(axis, rows):
    out = []
    for half in range(2 if axis == 0 else 1):
        lane = lax.broadcasted_iota(jnp.int32, (rows, LANES), 1)
        t = lax.shift_right_logical(lane, 4) + 8 * half if axis == 0 else jnp.bitwise_and(lane, 15)
        out.append(0.5 - 0.5 * unit((2.0 * t.astype(jnp.float32) + 1.0) / 64.0)[0])
    return out


def keep(table, *lead):
    def store(c, j, half, value):
        table[(*lead, c, j, half, 0)] = value[0]
        table[(*lead, c, j, half, 1)] = value[1]

    return store


def fill_early(own, slow, tab):
    nodes = (lane_nodes(0, 32), lane_nodes(1, 32))
    row = lax.broadcasted_iota(jnp.int32, (32, LANES), 0)
    for n in range(4):
        index = full_index(n, row)
        jbits = {m: bit_of(index, PLACE[m]) for m in range(n)}

        def one_key(key, carry, n=n, index=index, jbits=jbits):
            bbits = {m: bit_of(index, PLACE[m]) for m in (*range(n + 1, 4), 6, 7)}
            bbits[4] = bbits[5] = key
            level_table(n, 32, jbits, bbits, own, nodes[n % 2], slow, keep(tab, n, key))
            return carry

        lax.fori_loop(0, 2, one_key, 0)


def fill_middle(own, slow, tab4, tab5):
    row = lax.broadcasted_iota(jnp.int32, (64, LANES), 0)
    jbits = {m: bit_of(row, PLACE[m]) for m in range(4)}
    level_table(4, 64, jbits, {6: bit_of(row, PLACE[6])}, own, lane_nodes(0, 64), slow, keep(tab4))
    nodes = lane_nodes(1, 64)

    def five(j4, carry):
        bbits = {7: bit_of(row, PLACE[7])}
        level_table(5, 64, {**jbits, 4: j4}, bbits, own, nodes, slow, keep(tab5, j4))
        return carry

    lax.fori_loop(0, 2, five, 0)


def fill_late(own, slow, tab6, tab7, last):
    row32 = lax.broadcasted_iota(jnp.int32, (32, LANES), 0)
    six, seven = full_index(6, row32), full_index(7, row32)
    first_nodes, second_nodes = lane_nodes(0, 32), lane_nodes(1, 32)

    def rest(k, carry):
        j4, j5 = k // 2, lax.rem(k, 2)
        jbits = {m: bit_of(six, PLACE[m]) for m in range(4)}
        jbits.update({4: j4, 5: j5})
        level_table(6, 32, jbits, {}, own, first_nodes, slow, keep(tab6, k))
        jbits = {m: bit_of(seven, PLACE[m]) for m in (0, 1, 2, 3, 6)}
        jbits.update({4: j4, 5: j5})
        level_table(7, 32, jbits, {}, own, second_nodes, slow, keep(tab7, k))
        first = target_center(6, jbits, own)
        z2 = second_nodes[0]
        for j in range(2):
            second = target_center(7, {**jbits, 7: j}, own)
            tail = z2 * second[1] + shifts(z2, 1, slow) * second[2]
            for half in range(2):
                point = first_nodes[half]
                cos, sin = unit(point * first[0] + shifts(point, 0, slow) * first[2] + tail)
                last[k, j, half, 0] = cos
                last[k, j, half, 1] = sin
        return carry

    lax.fori_loop(0, 4, rest, 0)


def row_pattern(place):
    if place >= 3:
        return [k * 2 * 2**place for k in range(32 // 2**place)], 2**place, 1
    return list(range(2**place)), 32 >> place, 2 ** (place + 1)


def read_children(ref, lead, place):
    starts, size, stride = row_pattern(place)
    return [
        [
            [
                jnp.concatenate(
                    [
                        ref[(*lead, part, half, pl.ds(s + c * 2**place, size, stride=stride))]
                        for s in starts
                    ]
                )
                for half in range(2)
            ]
            for part in range(2)
        ]
        for c in range(2)
    ]


def write_siblings(ref, lead, place, out, at):
    starts, size, stride = row_pattern(place)
    for j in range(2):
        for part in range(2):
            for half in range(2):
                block = out(at, j, part, half)
                for k, s in enumerate(starts):
                    ref[(*lead, part, half, pl.ds(s + j * 2**place, size, stride=stride))] = block[
                        k * size : (k + 1) * size
                    ]


def phases_of(table, lead):
    return lambda c, j, half: (table[(*lead, c, j, half, 0)], table[(*lead, c, j, half, 1)])


def early_levels(groups, first, state, tab, even_ref, odd_ref):
    for n in range(4):
        blocks = []
        for b4, b5 in groups:
            g = 2 * b4 + b5
            if n == 0:
                children = [
                    [
                        [
                            first(b4, b5, c, part * 2 + half)
                            for half in range(2)
                        ]
                        for part in range(2)
                    ]
                    for c in range(2)
                ]
            else:
                children = read_children(state, (g,), PLACE[n])
            blocks.append((children, phases_of(tab, (n, b5 if n % 2 else b4))))
        out = merge(n, blocks, even_ref, odd_ref)
        for at, (b4, b5) in enumerate(groups):
            write_siblings(state, (2 * b4 + b5,), PLACE[n], out, at)


QUADS = [(j, part, half) for j in range(2) for part in range(2) for half in range(2)]


def whole(ref, *leads):
    return [
        [[ref[(*lead, part, half)] for half in range(2)] for part in range(2)] for lead in leads
    ]


def level_four(b5, state, mid, tab4, even_ref, odd_ref):
    out = merge(4, [(whole(state, (b5,), (2 + b5,)), phases_of(tab4, ()))], even_ref, odd_ref)
    for j, part, half in QUADS:
        mid[b5, j, part, half] = out(0, j, part, half)


def late_levels(mid, deep, tab5, tab6, tab7, last, fin, even_ref, odd_ref, o_ref):
    blocks = [(whole(mid, (0, j4), (1, j4)), phases_of(tab5, (j4,))) for j4 in range(2)]
    out = merge(5, blocks, even_ref, odd_ref)
    for j4 in range(2):
        for j, part, half in QUADS:
            deep[2 * j4 + j, part, half] = out(j4, j, part, half)
    blocks = [(read_children(deep, (k,), PLACE[6]), phases_of(tab6, (k,))) for k in range(4)]
    out = merge(6, blocks, even_ref, odd_ref)
    for k in range(4):
        write_siblings(deep, (k,), PLACE[6], out, k)
    blocks = [(read_children(deep, (k,), PLACE[7]), phases_of(tab7, (k,))) for k in range(4)]
    out = merge(7, blocks, even_ref, odd_ref)
    for k in range(4):
        for j in range(2):
            for half in range(2):
                cos, sin = last[k, j, half, 0], last[k, j, half, 1]
                re, im = out(k, j, 0, half), out(k, j, 1, half)
                for part, value in ((0, re * cos - im * sin), (1, re * sin + im * cos)):
                    for top in range(4):
                        base = top * 64 + (k // 2) * 32 + (k % 2) * 2 + j
                        fin[part, half, pl.ds(base, 8, stride=4), :] = value[
                            top * 8 : top * 8 + 8
                        ]
    for part in range(2):
        for half in range(2):
            o_ref[part, :, half * LANES : (half + 1) * LANES] = fin[part, half]


FAR_FIRST = (4, 3, 5, 2, 6, 1, 7)


def kernel(
    w_ref, slow_hbm, even_hbm, odd_hbm, o_ref,
    raw, swapped, relayed, packed, passing, r_ref, give, take, even_raw, odd_raw, even_ref, odd_ref, slow_ref,
    state, mid, deep, tab, tab4, tab5, tab6, tab7, last, fin,
    pair_send, pair_recv, own_sem, load_sem, ready, send, pass_recv, pass_send, recv,
    give_send, give_recv,
):
    x, y, z, core = chip()
    d = own_bits()
    xs = [along_x(x, k) for k in range(4)]
    ys = [along_y(y, k) for k in range(4)]
    zs = [along_z(z, k, core) for k in range(8)]
    plane = [(dx, dy) for dx in range(4) for dy in range(4) if (dx, dy) != (0, 0)]
    bar = pltpu.get_barrier_semaphore()

    def device(px, py, pz):
        return (px[0] + pz[0], py[0] + pz[1])

    sibling = (xs[0][0] + zs[0][0] + 1 - 2 * core, ys[0][0] + zs[0][1])

    def signal(sem, where):
        pl.semaphore_signal(sem, inc=1, device_id=where, device_id_type=MESH)

    for dz in FAR_FIRST:
        signal(bar, device(xs[0], ys[0], zs[dz]))
    signal(bar, sibling)
    for dx, dy in plane:
        signal(bar, device(xs[dx], ys[dy], zs[0]))
    mine = pltpu.make_async_copy(w_ref, raw, own_sem)
    mine.start()
    loads = [
        pltpu.make_async_copy(a, b, load_sem.at[k])
        for k, (a, b) in enumerate(
            [(slow_hbm, slow_ref), (even_hbm, even_raw), (odd_hbm, odd_raw)]
        )
    ]
    for load in loads:
        load.start()
    mine.wait()
    near_rows = [pl.multiple_of(b2 * 64 + d[4] * 32, 32) for b2 in range(2)]

    def lanes(half):
        return slice(half * LANES, (half + 1) * LANES)

    for row in near_rows:
        for to in range(2):
            for q in range(4):
                relayed[pl.ds(row * 8 + to * 4 + q, 32, stride=8), :] = raw[
                    q // 2, pl.ds(to * 128 + row, 32), lanes(q % 2)
                ]
    pl.semaphore_wait(bar, 23)
    for dx, dy in plane:
        signal(ready, device(xs[dx], ys[dy], zs[0]))
    swap = pltpu.make_async_remote_copy(
        src_ref=raw.at[:, pl.ds((1 - core) * 128, 128), :],
        dst_ref=swapped,
        send_sem=pair_send,
        recv_sem=pair_recv,
        device_id=sibling,
        device_id_type=MESH,
    )
    swap.start()

    group = 2 * d[4] + d[5]
    landing = group * 256 + tile_in_group(d) * 8
    z_place = (d[6] * 4 + d[1] * 2 + d[7]) * 8

    def tile(ref, px, py, pz):
        return ref.at[pl.ds((px[1] + py[1] + pz[2]) * 8, 8), :]

    def straight(ref, px, py, pz):
        pltpu.make_async_remote_copy(
            src_ref=tile(ref, px, py, pz),
            dst_ref=r_ref.at[pl.ds(landing, 8), :],
            send_sem=send,
            recv_sem=recv.at[group],
            device_id=device(px, py, pz),
            device_id_type=MESH,
        ).start()

    for dx in (2, 1, 3):
        spot = passing.at[pl.ds((dx - 1) * 64 + z_place, 8), :]
        for dz in FAR_FIRST:
            pltpu.make_async_remote_copy(
                src_ref=tile(relayed, xs[dx], ys[0], zs[dz]),
                dst_ref=spot,
                send_sem=send,
                recv_sem=pass_recv,
                device_id=device(xs[0], ys[0], zs[dz]),
                device_id_type=MESH,
            ).start()
        pltpu.make_async_copy(tile(relayed, xs[dx], ys[0], zs[0]), spot, pass_recv).start()
    for dz in FAR_FIRST:
        straight(relayed, xs[0], ys[0], zs[dz])
    pltpu.make_async_copy(
        tile(relayed, xs[0], ys[0], zs[0]), r_ref.at[pl.ds(landing, 8), :], recv.at[group]
    ).start()

    swap.wait()
    first_core = core == 0
    for q in range(4):
        ours = raw[q // 2, pl.ds(core * 128, 128), lanes(q % 2)]
        theirs = swapped[q // 2, :, lanes(q % 2)]
        packed[pl.ds(q, 128, stride=8), :] = jnp.where(first_core, ours, theirs)
        packed[pl.ds(4 + q, 128, stride=8), :] = jnp.where(first_core, theirs, ours)

    for load in loads:
        load.wait()
    even_ref[0:512, :], even_ref[512:1024, :] = high_low(even_raw[...])
    odd_ref[:, 0:LANES], odd_ref[:, LANES : 2 * LANES] = high_low(odd_raw[...])
    own = (
        d[0] * 8 + d[2] * 4 + d[4] * 2 + d[6],
        d[1] * 8 + d[3] * 4 + d[5] * 2 + d[7],
    )
    slow = [slow_ref[0], slow_ref[1], slow_ref[2]]
    fill_early(own, slow, tab)

    pl.semaphore_wait(ready, 15)

    def two_away(k, carry):
        px = along_x(x, 2 + k)
        for dz in (*FAR_FIRST, 0):
            straight(packed, px, ys[2], zs[dz])
        return carry

    def one_away(k, carry):
        px, py = along_x(x, 2 + lax.rem(k, 4)), along_y(y, 1 + 2 * (k // 4))
        for dz in (*FAR_FIRST, 0):
            straight(packed, px, py, zs[dz])
        return carry

    lax.fori_loop(0, 4, two_away, 0)
    lax.fori_loop(0, 8, one_away, 0)
    fill_middle(own, slow, tab4, tab5)
    pltpu.make_async_copy(passing, passing, pass_recv).wait()
    for dx in (2, 1, 3):
        for b6 in range(2):
            for b1 in range(2):
                from_row = (dx - 1) * 64 + b6 * 32 + b1 * 16
                to_row = group * 256 + (d[2] * 16 + b6 * 8 + b1 * 4 + d[3] * 2) * 8
                pltpu.make_async_remote_copy(
                    src_ref=passing.at[pl.ds(from_row, 16), :],
                    dst_ref=r_ref.at[pl.ds(to_row, 16), :],
                    send_sem=pass_send,
                    recv_sem=recv.at[group],
                    device_id=device(xs[dx], ys[0], zs[0]),
                    device_id_type=MESH,
                ).start()
    fill_late(own, slow, tab6, tab7, last)

    def arrive(g):
        block = r_ref.at[pl.ds(g * 256, 256), :]
        pltpu.make_async_copy(block, block, recv.at[g]).wait()

    def received(b4, b5, c, q):
        return r_ref[pl.ds((2 * b4 + b5) * 256 + c * 4 + q, 32, stride=8), :]

    arrive(group)
    for q in range(4):
        zero, one = received(d[4], d[5], 0, q), received(d[4], d[5], 1, q)
        take[core, q] = jnp.where(first_core, zero, one)
        give[q] = jnp.where(first_core, one, zero)
    trade = pltpu.make_async_remote_copy(
        src_ref=give,
        dst_ref=take.at[core],
        send_sem=give_send,
        recv_sem=give_recv,
        device_id=sibling,
        device_id_type=MESH,
    )
    trade.start()
    trade.wait()
    levels = (state, tab, even_ref, odd_ref)
    early_levels([(d[4], d[5])], lambda b4, b5, c, q: take[c, q], *levels)
    arrive(2 * d[4] + 1 - d[5])
    early_levels([(d[4], 1 - d[5])], received, *levels)

    def far(k, carry):
        y_from = lax.rem(y + 3 + 2 * k, 4)
        b4, b5 = lax.rem(y_from, 2), y_from // 2
        arrive(2 * b4 + b5)
        early_levels([(b4, b5)], received, *levels)
        level_four(b5, state, mid, tab4, even_ref, odd_ref)
        return carry

    lax.fori_loop(0, 2, far, 0)
    late_levels(mid, deep, tab5, tab6, tab7, last, fin, even_ref, odd_ref, o_ref)
    sent = packed.at[pl.ds(0, 992), :]
    pltpu.make_async_copy(sent, sent, send).wait()
    pltpu.make_async_copy(passing, passing, pass_send).wait()


def butterfly(weights, slowness_terms):
    hbm = pl.BlockSpec(memory_space=pltpu.HBM)
    f32, bf16 = jnp.float32, jnp.bfloat16
    return pl.pallas_call(
        kernel,
        out_shape=pltpu.VMEM((2, 256, 256), f32),
        in_specs=[hbm] * 4,
        out_specs=pl.BlockSpec(memory_space=pltpu.VMEM),
        scratch_shapes=[
            pltpu.VMEM((2, 256, 256), f32),
            pltpu.VMEM((2, 128, 256), f32),
            pltpu.VMEM((1024, LANES), f32),
            pltpu.VMEM((1024, LANES), f32),
            pltpu.VMEM((192, LANES), f32),
            pltpu.VMEM((1024, LANES), f32),
            pltpu.VMEM((4, 32, LANES), f32),
            pltpu.VMEM((2, 4, 32, LANES), f32),
            pltpu.VMEM((512, 256), f32),
            pltpu.VMEM((256, LANES), f32),
            pltpu.VMEM((1024, 256), bf16),
            pltpu.VMEM((256, 256), bf16),
            pltpu.SMEM((3,), f32),
            pltpu.VMEM((4, 2, 2, 64, LANES), f32),
            pltpu.VMEM((2, 2, 2, 2, 64, LANES), f32),
            pltpu.VMEM((4, 2, 2, 64, LANES), f32),
            pltpu.VMEM((4, 2, 2, 2, 2, 2, 32, LANES), f32),
            pltpu.VMEM((2, 2, 2, 2, 64, LANES), f32),
            pltpu.VMEM((2, 2, 2, 1, 2, 64, LANES), f32),
            pltpu.VMEM((4, 2, 2, 2, 2, 32, LANES), f32),
            pltpu.VMEM((4, 2, 2, 1, 2, 32, LANES), f32),
            pltpu.VMEM((4, 2, 2, 2, 32, LANES), f32),
            pltpu.VMEM((2, 2, 256, LANES), f32),
            pltpu.SemaphoreType.DMA,
            pltpu.SemaphoreType.DMA,
            pltpu.SemaphoreType.DMA,
            pltpu.SemaphoreType.DMA((3,)),
            pltpu.SemaphoreType.REGULAR,
            pltpu.SemaphoreType.DMA,
            pltpu.SemaphoreType.DMA,
            pltpu.SemaphoreType.DMA,
            pltpu.SemaphoreType.DMA((4,)),
            pltpu.SemaphoreType.DMA,
            pltpu.SemaphoreType.DMA,
        ],
        compiler_params=pltpu.CompilerParams(
            collective_id=0, has_side_effects=True, vmem_limit_bytes=48 * 2**20
        ),
    )(
        *(
            pltpu.with_memory_space_constraint(a, pltpu.HBM)
            for a in (
                weights,
                slowness_terms,
                jnp.asarray(even_matrix()),
                jnp.asarray(odd_matrix()),
            )
        )
    )


def local(weights, slowness_terms):
    return butterfly(weights.reshape(2, 256, 256), slowness_terms).reshape(weights.shape)


def solution(mesh):
    return jax.shard_map(
        local,
        mesh=mesh,
        in_specs=(P(None, "src", "tgt", None, None), P()),
        out_specs=P(None, "src", "tgt", None, None),
        check_vma=False,
    )
```

```python
import math

import jax
import jax.numpy as jnp
import numpy as np
from jax import lax
from jax.experimental import pallas as pl
from jax.experimental.pallas import tpu as pltpu
from jax.sharding import PartitionSpec as P

MESH = pl.DeviceIdType.MESH
NODES = 16
LANES = 128
PERIOD = 2.0 * math.pi


def nodes_np():
    t = np.arange(NODES, dtype=np.float64)
    return 0.5 - 0.5 * np.cos((2.0 * t + 1.0) * math.pi / (2 * NODES))


def merge_matrix(axis):
    z = nodes_np()
    eye = np.eye(NODES)
    blocks = []
    for c in range(2):
        at = (c + z) / 2.0
        lag = np.ones((NODES, NODES))
        for t in range(NODES):
            for m in range(NODES):
                if m != t:
                    lag[:, t] *= (at - z[m]) / (z[t] - z[m])
        if axis == 0:
            full = lag[:, None, :, None] * eye[None, :, None, :]
        else:
            full = eye[:, None, :, None] * lag[None, :, None, :]
        blocks.append(full.reshape(256, 256))
    return np.concatenate(blocks)


def even_matrix():
    return merge_matrix(0).astype(np.float32)


def odd_matrix():
    full = merge_matrix(1)
    block = np.concatenate([full[:LANES, :LANES], full[256 : 256 + LANES, :LANES]])
    return block.astype(np.float32)


def fit(fn, count):
    u = 0.125 - 0.125 * np.cos((np.arange(400) + 0.5) * math.pi / 400)
    c = np.polynomial.chebyshev.Chebyshev.fit(u, fn(np.sqrt(u)), count - 1, domain=[0, 0.25])
    return [float(v) for v in c.convert(kind=np.polynomial.Polynomial, domain=[-1, 1]).coef]


SIN_FIT = fit(lambda f: np.sin(math.pi * f) / f, 5)
COS_FIT = fit(lambda f: np.cos(math.pi * f), 6)


def horner(u, coef):
    acc = jnp.full_like(u, coef[-1])
    for v in coef[-2::-1]:
        acc = acc * u + v
    return acc


def unit(turns):
    f = turns - jnp.round(turns)
    u = f * f
    s = f * horner(u, SIN_FIT)
    c = horner(u, COS_FIT)
    return 1.0 - 2.0 * s * s, 2.0 * s * c


def own_bits():
    src, tgt = lax.axis_index("src"), lax.axis_index("tgt")
    bits = [lax.rem(src // 2**m, 2) for m in range(4)]
    return bits + [lax.rem(tgt // 2**m, 2) for m in range(4)]


def chip():
    src, tgt = lax.axis_index("src"), lax.axis_index("tgt")
    x, z_hi, core = src // 4, lax.rem(src // 2, 2), lax.rem(src, 2)
    return x, lax.rem(tgt, 4), z_hi * 4 + tgt // 4, core


def along_x(x, step):
    a = lax.rem(x + step, 4)
    return a * 4, lax.rem(a, 2) * 64 + (a // 2) * 4


def along_y(y, step):
    a = lax.rem(y + step, 4)
    return a, lax.rem(a, 2) * 32 + (a // 2) * 2


def along_z(z, step, core):
    a = lax.rem(z + step, 8)
    low, high = lax.rem(a, 4), a // 4
    return high * 2 + core, low * 4, lax.rem(low, 2) * 16 + high * 8 + low // 2


def tile_in_group(d):
    return d[2] * 16 + d[6] * 8 + d[1] * 4 + d[3] * 2 + d[7]


PLACE = {0: 5, 2: 4, 6: 3, 1: 2, 3: 1, 7: 0}


def bit_of(index, place):
    return jnp.bitwise_and(lax.shift_right_logical(index, place), 1)


def full_index(n, row):
    place = PLACE[n]
    if place >= 3:
        high = lax.shift_right_logical(row, place)
        return lax.shift_left(high, place + 1) + jnp.bitwise_and(row, 2**place - 1)
    per = 5 - place
    return lax.shift_left(jnp.bitwise_and(row, 2**per - 1), place + 1) + lax.shift_right_logical(row, per)


def center(own, js):
    total = own.astype(jnp.float32) * 16.0 - 128.0
    width = 16.0
    for j in js:
        width = width / 2.0
        total = total + (j.astype(jnp.float32) if hasattr(j, "astype") else float(j)) * width
    return total + width / 2.0


def target_center(n, jbits, own):
    first = center(own[0], [jbits[m] for m in range(0, n + 1, 2)])
    second = center(own[1], [jbits[m] for m in range(1, n + 1, 2)])
    return first, second, jnp.sqrt(first * first + second * second)


def shifts(point, axis, slow):
    cos, sin = unit(point)
    if axis == 0:
        return slow[0] + slow[1] * sin
    return slow[2] * cos


def flipped(bit, role):
    return bit + role - 2 * bit * role


def level_table(n, rows, jbits, bbits, own, z, slow, store, bit=0):
    axis = n % 2
    done = n // 2
    width = 2.0**done / 16.0
    corner = 0.0
    for m in range(n + 2, 8, 2):
        corner = corner + bbits[m].astype(jnp.float32) * (2.0 ** (m // 2) / 16.0)
    last = target_center(n - 2, jbits, own) if n >= 2 else None
    for j in range(2):
        jnew = dict(jbits)
        jnew[n] = j
        new = target_center(n, jnew, own)
        if last is None:
            step_k, step_r = -new[axis], -new[2]
        else:
            step_k, step_r = last[axis] - new[axis], last[2] - new[2]
        for half in range(2 if axis == 0 else 1):
            for c in range(2):
                child = flipped(bit, c)
                if not isinstance(child, int):
                    child = child.astype(jnp.float32)
                point = corner + width * (child + z[half])
                turns = point * step_k + shifts(point, axis, slow) * step_r
                store(c, j, half, unit(turns))


def halves_first(n, children, phases):
    out = []
    for j in range(2):
        real, imag = [], []
        for c in range(2):
            pairs = [phases(c, j, half if n % 2 == 0 else 0) for half in range(2)]
            re, im = children[c]
            real.append([re[h] * pairs[h][0] - im[h] * pairs[h][1] for h in range(2)])
            imag.append([re[h] * pairs[h][1] + im[h] * pairs[h][0] for h in range(2)])
        out.append((real, imag))
    return out


def high_low(full):
    high = full.astype(jnp.bfloat16)
    return high, (full - high.astype(jnp.float32)).astype(jnp.bfloat16)


def merge(n, blocks, even_ref, odd_ref):
    turned = [halves_first(n, *block) for block in blocks]
    rows = blocks[0][0][0][0][0].shape[0]
    f32 = jnp.float32
    if n % 2 == 0:
        full = jnp.concatenate(
            [
                jnp.concatenate([t[j][part][c][h] for c in range(2) for h in range(2)], axis=1)
                for t in turned
                for j in range(2)
                for part in range(2)
            ]
        )
        count = full.shape[0]
        high, low = high_low(full)
        both = jnp.dot(
            jnp.concatenate([high, low]), even_ref[0:512, :], preferred_element_type=f32
        )
        rest = jnp.dot(high, even_ref[512:1024, :], preferred_element_type=f32)
        total = both[:count] + (both[count:] + rest)

        def out(block, j, part, half):
            first = (block * 4 + 2 * j + part) * rows
            return total[first : first + rows, half * LANES : (half + 1) * LANES]

        return out
    full = jnp.concatenate(
        [
            jnp.concatenate([t[j][part][c][h] for c in range(2)], axis=1)
            for t in turned
            for j in range(2)
            for part in range(2)
            for h in range(2)
        ]
    )
    count = full.shape[0]
    high, low = high_low(full)
    both = jnp.dot(jnp.concatenate([high, low]), odd_ref[...], preferred_element_type=f32)
    total = both[:count, :LANES] + (both[:count, LANES:] + both[count:, :LANES])

    def out(block, j, part, half):
        first = (block * 8 + 4 * j + 2 * part + half) * rows
        return total[first : first + rows]

    return out


def lane_nodes(axis, rows):
    out = []
    for half in range(2 if axis == 0 else 1):
        lane = lax.broadcasted_iota(jnp.int32, (rows, LANES), 1)
        t = lax.shift_right_logical(lane, 4) + 8 * half if axis == 0 else jnp.bitwise_and(lane, 15)
        out.append(0.5 - 0.5 * unit((2.0 * t.astype(jnp.float32) + 1.0) / 64.0)[0])
    return out


def keep(table, *lead):
    def store(c, j, half, value):
        table[(*lead, c, j, half, 0)] = value[0]
        table[(*lead, c, j, half, 1)] = value[1]

    return store


def fill_early(d, own, slow, tab):
    nodes = (lane_nodes(0, 32), lane_nodes(1, 32))
    row = lax.broadcasted_iota(jnp.int32, (32, LANES), 0)
    for n in range(4):
        index = full_index(n, row)
        jbits = {m: bit_of(index, PLACE[m]) for m in range(n)}

        def one_role(role, carry, n=n, index=index, jbits=jbits):
            bbits = {m: bit_of(index, PLACE[m]) for m in (*range(n + 1, 4), 6, 7)}
            bbits[4], bbits[5] = flipped(d[4], role), flipped(d[5], role)
            level_table(n, 32, jbits, bbits, own, nodes[n % 2], slow, keep(tab, n, role))
            return carry

        lax.fori_loop(0, 2, one_role, 0)


def fill_middle(d, own, slow, tab4, tab5):
    row = lax.broadcasted_iota(jnp.int32, (64, LANES), 0)
    jbits = {m: bit_of(row, PLACE[m]) for m in range(4)}
    corner = {6: bit_of(row, PLACE[6])}
    level_table(4, 64, jbits, corner, own, lane_nodes(0, 64), slow, keep(tab4), d[4])
    nodes = lane_nodes(1, 64)

    def five(j4, carry):
        bbits = {7: bit_of(row, PLACE[7])}
        level_table(5, 64, {**jbits, 4: j4}, bbits, own, nodes, slow, keep(tab5, j4), d[5])
        return carry

    lax.fori_loop(0, 2, five, 0)


def fill_late(own, slow, tab6, tab7, last):
    row32 = lax.broadcasted_iota(jnp.int32, (32, LANES), 0)
    six, seven = full_index(6, row32), full_index(7, row32)
    first_nodes, second_nodes = lane_nodes(0, 32), lane_nodes(1, 32)

    def rest(k, carry):
        j4, j5 = k // 2, lax.rem(k, 2)
        jbits = {m: bit_of(six, PLACE[m]) for m in range(4)}
        jbits.update({4: j4, 5: j5})
        level_table(6, 32, jbits, {}, own, first_nodes, slow, keep(tab6, k))
        jbits = {m: bit_of(seven, PLACE[m]) for m in (0, 1, 2, 3, 6)}
        jbits.update({4: j4, 5: j5})
        level_table(7, 32, jbits, {}, own, second_nodes, slow, keep(tab7, k))
        first = target_center(6, jbits, own)
        z2 = second_nodes[0]
        for j in range(2):
            second = target_center(7, {**jbits, 7: j}, own)
            tail = z2 * second[1] + shifts(z2, 1, slow) * second[2]
            for half in range(2):
                point = first_nodes[half]
                cos, sin = unit(point * first[0] + shifts(point, 0, slow) * first[2] + tail)
                last[k, j, half, 0] = cos
                last[k, j, half, 1] = sin
        return carry

    lax.fori_loop(0, 4, rest, 0)


def row_pattern(place):
    if place >= 3:
        return [k * 2 * 2**place for k in range(32 // 2**place)], 2**place, 1
    return list(range(2**place)), 32 >> place, 2 ** (place + 1)


def read_children(ref, lead, place):
    starts, size, stride = row_pattern(place)
    return [
        [
            [
                jnp.concatenate(
                    [
                        ref[(*lead, part, half, pl.ds(s + c * 2**place, size, stride=stride))]
                        for s in starts
                    ]
                )
                for half in range(2)
            ]
            for part in range(2)
        ]
        for c in range(2)
    ]


def write_siblings(ref, lead, place, out, at):
    starts, size, stride = row_pattern(place)
    for j in range(2):
        for part in range(2):
            for half in range(2):
                block = out(at, j, part, half)
                for k, s in enumerate(starts):
                    ref[(*lead, part, half, pl.ds(s + j * 2**place, size, stride=stride))] = block[
                        k * size : (k + 1) * size
                    ]


def phases_of(table, lead):
    return lambda c, j, half: (table[(*lead, c, j, half, 0)], table[(*lead, c, j, half, 1)])


PLACES = ((0, 0), (0, 1), (1, 1), (1, 0))


def early_levels(groups, first, state, tab, even_ref, odd_ref):
    for n in range(4):
        blocks = []
        for g in groups:
            if n == 0:
                children = [
                    [[first(g, c, part * 2 + half) for half in range(2)] for part in range(2)]
                    for c in range(2)
                ]
            else:
                children = read_children(state, (g,), PLACE[n])
            blocks.append((children, phases_of(tab, (n, PLACES[g][n % 2]))))
        out = merge(n, blocks, even_ref, odd_ref)
        for at, g in enumerate(groups):
            write_siblings(state, (g,), PLACE[n], out, at)


QUADS = [(j, part, half) for j in range(2) for part in range(2) for half in range(2)]


def whole(ref, *leads):
    return [
        [[ref[(*lead, part, half)] for half in range(2)] for part in range(2)] for lead in leads
    ]


def level_four(near, far, state, mid, tab4, even_ref, odd_ref):
    out = merge(4, [(whole(state, (near,), (far,)), phases_of(tab4, ()))], even_ref, odd_ref)
    for j, part, half in QUADS:
        mid[near, j, part, half] = out(0, j, part, half)


def late_levels(mid, deep, tab5, tab6, tab7, last, fin, even_ref, odd_ref, odd5_ref, o_ref):
    blocks = [(whole(mid, (0, j4), (1, j4)), phases_of(tab5, (j4,))) for j4 in range(2)]
    out = merge(5, blocks, even_ref, odd5_ref)
    for j4 in range(2):
        for j, part, half in QUADS:
            deep[2 * j4 + j, part, half] = out(j4, j, part, half)
    blocks = [(read_children(deep, (k,), PLACE[6]), phases_of(tab6, (k,))) for k in range(4)]
    out = merge(6, blocks, even_ref, odd_ref)
    for k in range(4):
        write_siblings(deep, (k,), PLACE[6], out, k)
    blocks = [(read_children(deep, (k,), PLACE[7]), phases_of(tab7, (k,))) for k in range(4)]
    out = merge(7, blocks, even_ref, odd_ref)
    for k in range(4):
        for j in range(2):
            for half in range(2):
                cos, sin = last[k, j, half, 0], last[k, j, half, 1]
                re, im = out(k, j, 0, half), out(k, j, 1, half)
                for part, value in ((0, re * cos - im * sin), (1, re * sin + im * cos)):
                    for top in range(4):
                        base = top * 64 + (k // 2) * 32 + (k % 2) * 2 + j
                        fin[part, half, pl.ds(base, 8, stride=4), :] = value[
                            top * 8 : top * 8 + 8
                        ]
    for part in range(2):
        for half in range(2):
            o_ref[part, :, half * LANES : (half + 1) * LANES] = fin[part, half]


FAR_FIRST = (4, 3, 5, 2, 6, 1, 7)


def kernel(
    w_ref, slow_hbm, even_hbm, odd_hbm, o_ref,
    raw, swapped, relayed, packed, passing, r_ref, give, take, even_raw, odd_raw, even_ref, odd_ref,
    even4_ref, odd5_ref, slow_ref,
    state, mid, deep, tab, tab4, tab5, tab6, tab7, last, fin,
    pair_send, pair_recv, own_sem, load_sem, ready, send, pass_recv, pass_send, recv,
    give_send, give_recv,
):
    x, y, z, core = chip()
    d = own_bits()
    xs = [along_x(x, k) for k in range(4)]
    ys = [along_y(y, k) for k in range(4)]
    zs = [along_z(z, k, core) for k in range(8)]
    plane = [(dx, dy) for dx in range(4) for dy in range(4) if (dx, dy) != (0, 0)]
    bar = pltpu.get_barrier_semaphore()

    def device(px, py, pz):
        return (px[0] + pz[0], py[0] + pz[1])

    sibling = (xs[0][0] + zs[0][0] + 1 - 2 * core, ys[0][0] + zs[0][1])

    def signal(sem, where):
        pl.semaphore_signal(sem, inc=1, device_id=where, device_id_type=MESH)

    for dz in FAR_FIRST:
        signal(bar, device(xs[0], ys[0], zs[dz]))
    signal(bar, sibling)
    for dx, dy in plane:
        signal(bar, device(xs[dx], ys[dy], zs[0]))
    mine = pltpu.make_async_copy(w_ref, raw, own_sem)
    mine.start()
    loads = [
        pltpu.make_async_copy(a, b, load_sem.at[k])
        for k, (a, b) in enumerate(
            [(slow_hbm, slow_ref), (even_hbm, even_raw), (odd_hbm, odd_raw)]
        )
    ]
    for load in loads:
        load.start()
    mine.wait()
    near_rows = [pl.multiple_of(b2 * 64 + d[4] * 32, 32) for b2 in range(2)]

    def lanes(half):
        return slice(half * LANES, (half + 1) * LANES)

    for row in near_rows:
        for to in range(2):
            for q in range(4):
                relayed[pl.ds(row * 8 + to * 4 + q, 32, stride=8), :] = raw[
                    q // 2, pl.ds(to * 128 + row, 32), lanes(q % 2)
                ]
    pl.semaphore_wait(bar, 23)
    for dx, dy in plane:
        signal(ready, device(xs[dx], ys[dy], zs[0]))
    swap = pltpu.make_async_remote_copy(
        src_ref=raw.at[:, pl.ds((1 - core) * 128, 128), :],
        dst_ref=swapped,
        send_sem=pair_send,
        recv_sem=pair_recv,
        device_id=sibling,
        device_id_type=MESH,
    )
    swap.start()

    place = tile_in_group(d) * 8
    z_place = (d[6] * 4 + d[1] * 2 + d[7]) * 8

    def tile(ref, px, py, pz):
        return ref.at[pl.ds((px[1] + py[1] + pz[2]) * 8, 8), :]

    def straight(ref, g, px, py, pz):
        pltpu.make_async_remote_copy(
            src_ref=tile(ref, px, py, pz),
            dst_ref=r_ref.at[g, pl.ds(place, 8), :],
            send_sem=send,
            recv_sem=recv.at[g],
            device_id=device(px, py, pz),
            device_id_type=MESH,
        ).start()

    for dx in (2, 1, 3):
        spot = passing.at[pl.ds((dx - 1) * 64 + z_place, 8), :]
        for dz in FAR_FIRST:
            pltpu.make_async_remote_copy(
                src_ref=tile(relayed, xs[dx], ys[0], zs[dz]),
                dst_ref=spot,
                send_sem=send,
                recv_sem=pass_recv,
                device_id=device(xs[0], ys[0], zs[dz]),
                device_id_type=MESH,
            ).start()
        pltpu.make_async_copy(tile(relayed, xs[dx], ys[0], zs[0]), spot, pass_recv).start()
    for dz in FAR_FIRST:
        straight(relayed, 0, xs[0], ys[0], zs[dz])
    pltpu.make_async_copy(
        tile(relayed, xs[0], ys[0], zs[0]), r_ref.at[0, pl.ds(place, 8), :], recv.at[0]
    ).start()

    swap.wait()
    first_core = core == 0
    for q in range(4):
        ours = raw[q // 2, pl.ds(core * 128, 128), lanes(q % 2)]
        theirs = swapped[q // 2, :, lanes(q % 2)]
        packed[pl.ds(q, 128, stride=8), :] = jnp.where(first_core, ours, theirs)
        packed[pl.ds(4 + q, 128, stride=8), :] = jnp.where(first_core, theirs, ours)

    for load in loads:
        load.wait()
    even_ref[0:512, :], even_ref[512:1024, :] = high_low(even_raw[...])
    odd_ref[:, 0:LANES], odd_ref[:, LANES : 2 * LANES] = high_low(odd_raw[...])
    for c in range(2):
        child = pl.multiple_of(flipped(d[4], c) * 256, 256)
        high, low = high_low(even_raw[pl.ds(child, 256), :])
        even4_ref[c * 256 : c * 256 + 256, :] = high
        even4_ref[512 + c * 256 : 768 + c * 256, :] = low
        child = pl.multiple_of(flipped(d[5], c) * LANES, LANES)
        high, low = high_low(odd_raw[pl.ds(child, LANES), :])
        odd5_ref[c * LANES : (c + 1) * LANES, 0:LANES] = high
        odd5_ref[c * LANES : (c + 1) * LANES, LANES : 2 * LANES] = low
    own = (
        d[0] * 8 + d[2] * 4 + d[4] * 2 + d[6],
        d[1] * 8 + d[3] * 4 + d[5] * 2 + d[7],
    )
    slow = [slow_ref[0], slow_ref[1], slow_ref[2]]

    pl.semaphore_wait(ready, 15)

    def two_away(k, carry):
        px = along_x(x, 2 + k)
        for dz in (*FAR_FIRST, 0):
            straight(packed, 1, px, ys[2], zs[dz])
        return carry

    def one_away(k, carry):
        px = along_x(x, 2 + lax.rem(k, 4))
        py = along_y(y, 1 + 2 * flipped(1 - lax.rem(y, 2), k // 4))
        for dz in (*FAR_FIRST, 0):
            straight(packed, 2 + k // 4, px, py, zs[dz])
        return carry

    lax.fori_loop(0, 4, two_away, 0)
    pltpu.make_async_copy(passing, passing, pass_recv).wait()
    for dx in (2, 1, 3):
        for b6 in range(2):
            for b1 in range(2):
                from_row = (dx - 1) * 64 + b6 * 32 + b1 * 16
                to_row = (d[2] * 16 + b6 * 8 + b1 * 4 + d[3] * 2) * 8
                pltpu.make_async_remote_copy(
                    src_ref=passing.at[pl.ds(from_row, 16), :],
                    dst_ref=r_ref.at[0, pl.ds(to_row, 16), :],
                    send_sem=pass_send,
                    recv_sem=recv.at[0],
                    device_id=device(xs[dx], ys[0], zs[0]),
                    device_id_type=MESH,
                ).start()
    lax.fori_loop(0, 8, one_away, 0)
    fill_early(d, own, slow, tab)
    fill_middle(d, own, slow, tab4, tab5)
    fill_late(own, slow, tab6, tab7, last)

    def arrive(g):
        pltpu.make_async_copy(r_ref.at[g], r_ref.at[g], recv.at[g]).wait()

    def received(g, c, q):
        return r_ref[g, pl.ds(c * 4 + q, 32, stride=8), :]

    def near(g, c, q):
        return take[c, q] if g == 0 else received(g, c, q)

    arrive(0)
    for q in range(4):
        zero, one = received(0, 0, q), received(0, 1, q)
        take[core, q] = jnp.where(first_core, zero, one)
        give[q] = jnp.where(first_core, one, zero)
    trade = pltpu.make_async_remote_copy(
        src_ref=give,
        dst_ref=take.at[core],
        send_sem=give_send,
        recv_sem=give_recv,
        device_id=sibling,
        device_id_type=MESH,
    )
    trade.start()
    trade.wait()
    arrive(1)
    levels = (state, tab, even_ref, odd_ref)
    early_levels([0, 1], near, *levels)
    arrive(2)
    early_levels([2], received, *levels)
    level_four(1, 2, state, mid, tab4, even4_ref, odd_ref)
    arrive(3)
    early_levels([3], received, *levels)
    level_four(0, 3, state, mid, tab4, even4_ref, odd_ref)
    late_levels(mid, deep, tab5, tab6, tab7, last, fin, even_ref, odd_ref, odd5_ref, o_ref)
    sent = packed.at[pl.ds(0, 992), :]
    pltpu.make_async_copy(sent, sent, send).wait()
    pltpu.make_async_copy(passing, passing, pass_send).wait()


def butterfly(weights, slowness_terms):
    hbm = pl.BlockSpec(memory_space=pltpu.HBM)
    f32, bf16 = jnp.float32, jnp.bfloat16
    return pl.pallas_call(
        kernel,
        out_shape=pltpu.VMEM((2, 256, 256), f32),
        in_specs=[hbm] * 4,
        out_specs=pl.BlockSpec(memory_space=pltpu.VMEM),
        scratch_shapes=[
            pltpu.VMEM((2, 256, 256), f32),
            pltpu.VMEM((2, 128, 256), f32),
            pltpu.VMEM((1024, LANES), f32),
            pltpu.VMEM((1024, LANES), f32),
            pltpu.VMEM((192, LANES), f32),
            pltpu.VMEM((4, 256, LANES), f32),
            pltpu.VMEM((4, 32, LANES), f32),
            pltpu.VMEM((2, 4, 32, LANES), f32),
            pltpu.VMEM((512, 256), f32),
            pltpu.VMEM((256, LANES), f32),
            pltpu.VMEM((1024, 256), bf16),
            pltpu.VMEM((256, 256), bf16),
            pltpu.VMEM((1024, 256), bf16),
            pltpu.VMEM((256, 256), bf16),
            pltpu.SMEM((3,), f32),
            pltpu.VMEM((4, 2, 2, 64, LANES), f32),
            pltpu.VMEM((2, 2, 2, 2, 64, LANES), f32),
            pltpu.VMEM((4, 2, 2, 64, LANES), f32),
            pltpu.VMEM((4, 2, 2, 2, 2, 2, 32, LANES), f32),
            pltpu.VMEM((2, 2, 2, 2, 64, LANES), f32),
            pltpu.VMEM((2, 2, 2, 1, 2, 64, LANES), f32),
            pltpu.VMEM((4, 2, 2, 2, 2, 32, LANES), f32),
            pltpu.VMEM((4, 2, 2, 1, 2, 32, LANES), f32),
            pltpu.VMEM((4, 2, 2, 2, 32, LANES), f32),
            pltpu.VMEM((2, 2, 256, LANES), f32),
            pltpu.SemaphoreType.DMA,
            pltpu.SemaphoreType.DMA,
            pltpu.SemaphoreType.DMA,
            pltpu.SemaphoreType.DMA((3,)),
            pltpu.SemaphoreType.REGULAR,
            pltpu.SemaphoreType.DMA,
            pltpu.SemaphoreType.DMA,
            pltpu.SemaphoreType.DMA,
            pltpu.SemaphoreType.DMA((4,)),
            pltpu.SemaphoreType.DMA,
            pltpu.SemaphoreType.DMA,
        ],
        compiler_params=pltpu.CompilerParams(
            collective_id=0, has_side_effects=True, vmem_limit_bytes=48 * 2**20
        ),
    )(
        *(
            pltpu.with_memory_space_constraint(a, pltpu.HBM)
            for a in (
                weights,
                slowness_terms,
                jnp.asarray(even_matrix()),
                jnp.asarray(odd_matrix()),
            )
        )
    )


def local(weights, slowness_terms):
    return butterfly(weights.reshape(2, 256, 256), slowness_terms).reshape(weights.shape)


def solution(mesh):
    return jax.shard_map(
        local,
        mesh=mesh,
        in_specs=(P(None, "src", "tgt", None, None), P()),
        out_specs=P(None, "src", "tgt", None, None),
        check_vma=False,
    )
```

```python
import math

import jax
import jax.numpy as jnp
import numpy as np
from jax import lax
from jax.experimental import pallas as pl
from jax.experimental.pallas import tpu as pltpu
from jax.sharding import PartitionSpec as P

MESH = pl.DeviceIdType.MESH
NODES = 16
LANES = 128
PERIOD = 2.0 * math.pi


def nodes_np():
    t = np.arange(NODES, dtype=np.float64)
    return 0.5 - 0.5 * np.cos((2.0 * t + 1.0) * math.pi / (2 * NODES))


def merge_matrix(axis):
    z = nodes_np()
    eye = np.eye(NODES)
    blocks = []
    for c in range(2):
        at = (c + z) / 2.0
        lag = np.ones((NODES, NODES))
        for t in range(NODES):
            for m in range(NODES):
                if m != t:
                    lag[:, t] *= (at - z[m]) / (z[t] - z[m])
        if axis == 0:
            full = lag[:, None, :, None] * eye[None, :, None, :]
        else:
            full = eye[:, None, :, None] * lag[None, :, None, :]
        blocks.append(full.reshape(256, 256))
    return np.concatenate(blocks)


def even_matrix():
    return merge_matrix(0).astype(np.float32)


def odd_matrix():
    full = merge_matrix(1)
    block = np.concatenate([full[:LANES, :LANES], full[256 : 256 + LANES, :LANES]])
    return block.astype(np.float32)


def fit(fn, count):
    u = 0.125 - 0.125 * np.cos((np.arange(400) + 0.5) * math.pi / 400)
    c = np.polynomial.chebyshev.Chebyshev.fit(u, fn(np.sqrt(u)), count - 1, domain=[0, 0.25])
    return [float(v) for v in c.convert(kind=np.polynomial.Polynomial, domain=[-1, 1]).coef]


SIN_FIT = fit(lambda f: np.sin(math.pi * f) / f, 5)
COS_FIT = fit(lambda f: np.cos(math.pi * f), 6)


def horner(u, coef):
    acc = jnp.full_like(u, coef[-1])
    for v in coef[-2::-1]:
        acc = acc * u + v
    return acc


def unit(turns):
    f = turns - jnp.round(turns)
    u = f * f
    s = f * horner(u, SIN_FIT)
    c = horner(u, COS_FIT)
    return 1.0 - 2.0 * s * s, 2.0 * s * c


def own_bits():
    src, tgt = lax.axis_index("src"), lax.axis_index("tgt")
    bits = [lax.rem(src // 2**m, 2) for m in range(4)]
    return bits + [lax.rem(tgt // 2**m, 2) for m in range(4)]


def chip():
    src, tgt = lax.axis_index("src"), lax.axis_index("tgt")
    x, z_hi, core = src // 4, lax.rem(src // 2, 2), lax.rem(src, 2)
    return x, lax.rem(tgt, 4), z_hi * 4 + tgt // 4, core


def along_x(x, step):
    a = lax.rem(x + step, 4)
    return a * 4, lax.rem(a, 2) * 64 + (a // 2) * 4


def along_y(y, step):
    a = lax.rem(y + step, 4)
    return a, lax.rem(a, 2) * 32 + (a // 2) * 2


def along_z(z, step, core):
    a = lax.rem(z + step, 8)
    low, high = lax.rem(a, 4), a // 4
    return high * 2 + core, low * 4, lax.rem(low, 2) * 16 + high * 8 + low // 2


def tile_in_group(d):
    return d[2] * 16 + d[6] * 8 + d[1] * 4 + d[3] * 2 + d[7]


PLACE = {0: 5, 2: 4, 6: 3, 1: 2, 3: 1, 7: 0}


def bit_of(index, place):
    return jnp.bitwise_and(lax.shift_right_logical(index, place), 1)


def full_index(n, row):
    place = PLACE[n]
    if place >= 3:
        high = lax.shift_right_logical(row, place)
        return lax.shift_left(high, place + 1) + jnp.bitwise_and(row, 2**place - 1)
    per = 5 - place
    return lax.shift_left(jnp.bitwise_and(row, 2**per - 1), place + 1) + lax.shift_right_logical(row, per)


def center(own, js):
    total = own.astype(jnp.float32) * 16.0 - 128.0
    width = 16.0
    for j in js:
        width = width / 2.0
        total = total + (j.astype(jnp.float32) if hasattr(j, "astype") else float(j)) * width
    return total + width / 2.0


def target_center(n, jbits, own):
    first = center(own[0], [jbits[m] for m in range(0, n + 1, 2)])
    second = center(own[1], [jbits[m] for m in range(1, n + 1, 2)])
    return first, second, jnp.sqrt(first * first + second * second)


def shifts(point, axis, slow):
    cos, sin = unit(point)
    if axis == 0:
        return slow[0] + slow[1] * sin
    return slow[2] * cos


def flipped(bit, role):
    return bit + role - 2 * bit * role


def level_table(n, rows, jbits, bbits, own, z, slow, store, bit=0):
    axis = n % 2
    done = n // 2
    width = 2.0**done / 16.0
    corner = 0.0
    for m in range(n + 2, 8, 2):
        corner = corner + bbits[m].astype(jnp.float32) * (2.0 ** (m // 2) / 16.0)
    last = target_center(n - 2, jbits, own) if n >= 2 else None
    for j in range(2):
        jnew = dict(jbits)
        jnew[n] = j
        new = target_center(n, jnew, own)
        if last is None:
            step_k, step_r = -new[axis], -new[2]
        else:
            step_k, step_r = last[axis] - new[axis], last[2] - new[2]
        for half in range(2 if axis == 0 else 1):
            for c in range(2):
                child = flipped(bit, c)
                if not isinstance(child, int):
                    child = child.astype(jnp.float32)
                point = corner + width * (child + z[half])
                turns = point * step_k + shifts(point, axis, slow) * step_r
                store(c, j, half, unit(turns))


def halves_first(n, children, phases):
    out = []
    for j in range(2):
        real, imag = [], []
        for c in range(2):
            pairs = [phases(c, j, half if n % 2 == 0 else 0) for half in range(2)]
            re, im = children[c]
            real.append([re[h] * pairs[h][0] - im[h] * pairs[h][1] for h in range(2)])
            imag.append([re[h] * pairs[h][1] + im[h] * pairs[h][0] for h in range(2)])
        out.append((real, imag))
    return out


def high_low(full):
    high = full.astype(jnp.bfloat16)
    return high, (full - high.astype(jnp.float32)).astype(jnp.bfloat16)


def merge(n, blocks, even_ref, odd_ref):
    turned = [halves_first(n, *block) for block in blocks]
    rows = blocks[0][0][0][0][0].shape[0]
    f32 = jnp.float32
    if n % 2 == 0:
        full = jnp.concatenate(
            [
                jnp.concatenate([t[j][part][c][h] for c in range(2) for h in range(2)], axis=1)
                for t in turned
                for j in range(2)
                for part in range(2)
            ]
        )
        count = full.shape[0]
        high, low = high_low(full)
        total = jnp.dot(
            jnp.concatenate([high, high, low], axis=1),
            jnp.concatenate([even_ref[...], even_ref[0:512, :]]),
            preferred_element_type=f32,
        )

        def out(block, j, part, half):
            first = (block * 4 + 2 * j + part) * rows
            return total[first : first + rows, half * LANES : (half + 1) * LANES]

        return out
    full = jnp.concatenate(
        [
            jnp.concatenate([t[j][part][c][h] for c in range(2)], axis=1)
            for t in turned
            for j in range(2)
            for part in range(2)
            for h in range(2)
        ]
    )
    count = full.shape[0]
    high, low = high_low(full)
    both = jnp.dot(jnp.concatenate([high, low]), odd_ref[...], preferred_element_type=f32)
    total = both[:count, :LANES] + (both[:count, LANES:] + both[count:, :LANES])

    def out(block, j, part, half):
        first = (block * 8 + 4 * j + 2 * part + half) * rows
        return total[first : first + rows]

    return out


def lane_nodes(axis, rows):
    out = []
    for half in range(2 if axis == 0 else 1):
        lane = lax.broadcasted_iota(jnp.int32, (rows, LANES), 1)
        t = lax.shift_right_logical(lane, 4) + 8 * half if axis == 0 else jnp.bitwise_and(lane, 15)
        out.append(0.5 - 0.5 * unit((2.0 * t.astype(jnp.float32) + 1.0) / 64.0)[0])
    return out


def keep(table, *lead):
    def store(c, j, half, value):
        table[(*lead, c, j, half, 0)] = value[0]
        table[(*lead, c, j, half, 1)] = value[1]

    return store


def fill_early(d, own, slow, tab):
    nodes = (lane_nodes(0, 32), lane_nodes(1, 32))
    row = lax.broadcasted_iota(jnp.int32, (32, LANES), 0)
    for n in range(4):
        index = full_index(n, row)
        jbits = {m: bit_of(index, PLACE[m]) for m in range(n)}

        def one_role(role, carry, n=n, index=index, jbits=jbits):
            bbits = {m: bit_of(index, PLACE[m]) for m in (*range(n + 1, 4), 6, 7)}
            bbits[4], bbits[5] = flipped(d[4], role), flipped(d[5], role)
            level_table(n, 32, jbits, bbits, own, nodes[n % 2], slow, keep(tab, n, role))
            return carry

        lax.fori_loop(0, 2, one_role, 0)


def fill_middle(d, own, slow, tab4, tab5):
    row = lax.broadcasted_iota(jnp.int32, (64, LANES), 0)
    jbits = {m: bit_of(row, PLACE[m]) for m in range(4)}
    corner = {6: bit_of(row, PLACE[6])}
    level_table(4, 64, jbits, corner, own, lane_nodes(0, 64), slow, keep(tab4), d[4])
    nodes = lane_nodes(1, 64)

    def five(j4, carry):
        bbits = {7: bit_of(row, PLACE[7])}
        level_table(5, 64, {**jbits, 4: j4}, bbits, own, nodes, slow, keep(tab5, j4), d[5])
        return carry

    lax.fori_loop(0, 2, five, 0)


def fill_late(own, slow, tab6, tab7, last):
    row32 = lax.broadcasted_iota(jnp.int32, (32, LANES), 0)
    six, seven = full_index(6, row32), full_index(7, row32)
    first_nodes, second_nodes = lane_nodes(0, 32), lane_nodes(1, 32)

    def rest(k, carry):
        j4, j5 = k // 2, lax.rem(k, 2)
        jbits = {m: bit_of(six, PLACE[m]) for m in range(4)}
        jbits.update({4: j4, 5: j5})
        level_table(6, 32, jbits, {}, own, first_nodes, slow, keep(tab6, k))
        jbits = {m: bit_of(seven, PLACE[m]) for m in (0, 1, 2, 3, 6)}
        jbits.update({4: j4, 5: j5})
        level_table(7, 32, jbits, {}, own, second_nodes, slow, keep(tab7, k))
        first = target_center(6, jbits, own)
        z2 = second_nodes[0]
        for j in range(2):
            second = target_center(7, {**jbits, 7: j}, own)
            tail = z2 * second[1] + shifts(z2, 1, slow) * second[2]
            for half in range(2):
                point = first_nodes[half]
                cos, sin = unit(point * first[0] + shifts(point, 0, slow) * first[2] + tail)
                last[k, j, half, 0] = cos
                last[k, j, half, 1] = sin
        return carry

    lax.fori_loop(0, 4, rest, 0)


def row_pattern(place):
    if place >= 3:
        return [k * 2 * 2**place for k in range(32 // 2**place)], 2**place, 1
    return list(range(2**place)), 32 >> place, 2 ** (place + 1)


def read_children(ref, lead, place):
    starts, size, stride = row_pattern(place)
    return [
        [
            [
                jnp.concatenate(
                    [
                        ref[(*lead, part, half, pl.ds(s + c * 2**place, size, stride=stride))]
                        for s in starts
                    ]
                )
                for half in range(2)
            ]
            for part in range(2)
        ]
        for c in range(2)
    ]


def write_siblings(ref, lead, place, out, at):
    starts, size, stride = row_pattern(place)
    for j in range(2):
        for part in range(2):
            for half in range(2):
                block = out(at, j, part, half)
                for k, s in enumerate(starts):
                    ref[(*lead, part, half, pl.ds(s + j * 2**place, size, stride=stride))] = block[
                        k * size : (k + 1) * size
                    ]


def phases_of(table, lead):
    return lambda c, j, half: (table[(*lead, c, j, half, 0)], table[(*lead, c, j, half, 1)])


PLACES = ((0, 0), (0, 1), (1, 1), (1, 0))


def early_levels(groups, first, state, tab, even_ref, odd_ref):
    for n in range(4):
        blocks = []
        for g in groups:
            if n == 0:
                children = [
                    [[first(g, c, part * 2 + half) for half in range(2)] for part in range(2)]
                    for c in range(2)
                ]
            else:
                children = read_children(state, (g,), PLACE[n])
            blocks.append((children, phases_of(tab, (n, PLACES[g][n % 2]))))
        out = merge(n, blocks, even_ref, odd_ref)
        for at, g in enumerate(groups):
            write_siblings(state, (g,), PLACE[n], out, at)


QUADS = [(j, part, half) for j in range(2) for part in range(2) for half in range(2)]


def whole(ref, *leads):
    return [
        [[ref[(*lead, part, half)] for half in range(2)] for part in range(2)] for lead in leads
    ]


def level_four(near, far, state, mid, tab4, even_ref, odd_ref):
    out = merge(4, [(whole(state, (near,), (far,)), phases_of(tab4, ()))], even_ref, odd_ref)
    for j, part, half in QUADS:
        mid[near, j, part, half] = out(0, j, part, half)


def late_levels(mid, deep, tab5, tab6, tab7, last, fin, even_ref, odd_ref, odd5_ref, o_ref):
    blocks = [(whole(mid, (0, j4), (1, j4)), phases_of(tab5, (j4,))) for j4 in range(2)]
    out = merge(5, blocks, even_ref, odd5_ref)
    for j4 in range(2):
        for j, part, half in QUADS:
            deep[2 * j4 + j, part, half] = out(j4, j, part, half)
    blocks = [(read_children(deep, (k,), PLACE[6]), phases_of(tab6, (k,))) for k in range(4)]
    out = merge(6, blocks, even_ref, odd_ref)
    for k in range(4):
        write_siblings(deep, (k,), PLACE[6], out, k)
    blocks = [(read_children(deep, (k,), PLACE[7]), phases_of(tab7, (k,))) for k in range(4)]
    out = merge(7, blocks, even_ref, odd_ref)
    for k in range(4):
        for j in range(2):
            for half in range(2):
                cos, sin = last[k, j, half, 0], last[k, j, half, 1]
                re, im = out(k, j, 0, half), out(k, j, 1, half)
                for part, value in ((0, re * cos - im * sin), (1, re * sin + im * cos)):
                    for top in range(4):
                        base = top * 64 + (k // 2) * 32 + (k % 2) * 2 + j
                        fin[part, half, pl.ds(base, 8, stride=4), :] = value[
                            top * 8 : top * 8 + 8
                        ]
    for part in range(2):
        for half in range(2):
            o_ref[part, :, half * LANES : (half + 1) * LANES] = fin[part, half]


FAR_FIRST = (4, 3, 5, 2, 6, 1, 7)


def kernel(
    w_ref, slow_hbm, even_hbm, odd_hbm, o_ref,
    raw, swapped, relayed, packed, passing, r_ref, give, take, even_raw, odd_raw, even_ref, odd_ref,
    even4_ref, odd5_ref, slow_ref,
    state, mid, deep, tab, tab4, tab5, tab6, tab7, last, fin,
    pair_send, pair_recv, own_sem, load_sem, ready, send, pass_recv, pass_send, recv,
    give_send, give_recv,
):
    x, y, z, core = chip()
    d = own_bits()
    xs = [along_x(x, k) for k in range(4)]
    ys = [along_y(y, k) for k in range(4)]
    zs = [along_z(z, k, core) for k in range(8)]
    plane = [(dx, dy) for dx in range(4) for dy in range(4) if (dx, dy) != (0, 0)]
    bar = pltpu.get_barrier_semaphore()

    def device(px, py, pz):
        return (px[0] + pz[0], py[0] + pz[1])

    sibling = (xs[0][0] + zs[0][0] + 1 - 2 * core, ys[0][0] + zs[0][1])

    def signal(sem, where):
        pl.semaphore_signal(sem, inc=1, device_id=where, device_id_type=MESH)

    for dx, dy in plane:
        signal(bar, device(xs[dx], ys[dy], zs[0]))
    for dz in FAR_FIRST:
        signal(bar, device(xs[0], ys[0], zs[dz]))
    signal(bar, sibling)
    mine = pltpu.make_async_copy(w_ref, raw, own_sem)
    mine.start()
    loads = [
        pltpu.make_async_copy(a, b, load_sem.at[k])
        for k, (a, b) in enumerate(
            [(slow_hbm, slow_ref), (even_hbm, even_raw), (odd_hbm, odd_raw)]
        )
    ]
    for load in loads:
        load.start()
    mine.wait()
    near_rows = [pl.multiple_of(b2 * 64 + d[4] * 32, 32) for b2 in range(2)]

    def lanes(half):
        return slice(half * LANES, (half + 1) * LANES)

    for row in near_rows:
        for to in range(2):
            for q in range(4):
                relayed[pl.ds(row * 8 + to * 4 + q, 32, stride=8), :] = raw[
                    q // 2, pl.ds(to * 128 + row, 32), lanes(q % 2)
                ]
    pl.semaphore_wait(bar, 23)
    for dx, dy in plane:
        signal(ready, device(xs[dx], ys[dy], zs[0]))
    swap = pltpu.make_async_remote_copy(
        src_ref=raw.at[:, pl.ds((1 - core) * 128, 128), :],
        dst_ref=swapped,
        send_sem=pair_send,
        recv_sem=pair_recv,
        device_id=sibling,
        device_id_type=MESH,
    )
    swap.start()

    place = tile_in_group(d) * 8
    z_place = (d[6] * 4 + d[1] * 2 + d[7]) * 8

    def tile(ref, px, py, pz):
        return ref.at[pl.ds((px[1] + py[1] + pz[2]) * 8, 8), :]

    def straight(ref, g, px, py, pz):
        pltpu.make_async_remote_copy(
            src_ref=tile(ref, px, py, pz),
            dst_ref=r_ref.at[g, pl.ds(place, 8), :],
            send_sem=send,
            recv_sem=recv.at[g],
            device_id=device(px, py, pz),
            device_id_type=MESH,
        ).start()

    for dx in (2, 1, 3):
        spot = passing.at[pl.ds((dx - 1) * 64 + z_place, 8), :]
        for dz in FAR_FIRST:
            pltpu.make_async_remote_copy(
                src_ref=tile(relayed, xs[dx], ys[0], zs[dz]),
                dst_ref=spot,
                send_sem=send,
                recv_sem=pass_recv,
                device_id=device(xs[0], ys[0], zs[dz]),
                device_id_type=MESH,
            ).start()
        pltpu.make_async_copy(tile(relayed, xs[dx], ys[0], zs[0]), spot, pass_recv).start()
    for dz in FAR_FIRST:
        straight(relayed, 0, xs[0], ys[0], zs[dz])
    pltpu.make_async_copy(
        tile(relayed, xs[0], ys[0], zs[0]), r_ref.at[0, pl.ds(place, 8), :], recv.at[0]
    ).start()

    swap.wait()
    first_core = core == 0
    for q in range(4):
        ours = raw[q // 2, pl.ds(core * 128, 128), lanes(q % 2)]
        theirs = swapped[q // 2, :, lanes(q % 2)]
        packed[pl.ds(q, 128, stride=8), :] = jnp.where(first_core, ours, theirs)
        packed[pl.ds(4 + q, 128, stride=8), :] = jnp.where(first_core, theirs, ours)

    for load in loads:
        load.wait()
    even_ref[0:512, :], even_ref[512:1024, :] = high_low(even_raw[...])
    odd_ref[:, 0:LANES], odd_ref[:, LANES : 2 * LANES] = high_low(odd_raw[...])
    for c in range(2):
        child = pl.multiple_of(flipped(d[4], c) * 256, 256)
        high, low = high_low(even_raw[pl.ds(child, 256), :])
        even4_ref[c * 256 : c * 256 + 256, :] = high
        even4_ref[512 + c * 256 : 768 + c * 256, :] = low
        child = pl.multiple_of(flipped(d[5], c) * LANES, LANES)
        high, low = high_low(odd_raw[pl.ds(child, LANES), :])
        odd5_ref[c * LANES : (c + 1) * LANES, 0:LANES] = high
        odd5_ref[c * LANES : (c + 1) * LANES, LANES : 2 * LANES] = low
    own = (
        d[0] * 8 + d[2] * 4 + d[4] * 2 + d[6],
        d[1] * 8 + d[3] * 4 + d[5] * 2 + d[7],
    )
    slow = [slow_ref[0], slow_ref[1], slow_ref[2]]

    pl.semaphore_wait(ready, 15)

    def two_away(k, carry):
        px = along_x(x, 2 + k)
        for dz in (*FAR_FIRST, 0):
            straight(packed, 1, px, ys[2], zs[dz])
        return carry

    def one_away(k, carry):
        px = along_x(x, 2 + lax.rem(k, 4))
        py = along_y(y, 1 + 2 * flipped(1 - lax.rem(y, 2), k // 4))
        for dz in (*FAR_FIRST, 0):
            straight(packed, 2 + k // 4, px, py, zs[dz])
        return carry

    lax.fori_loop(0, 4, two_away, 0)
    pltpu.make_async_copy(passing, passing, pass_recv).wait()
    for dx in (2, 1, 3):
        for b6 in range(2):
            for b1 in range(2):
                from_row = (dx - 1) * 64 + b6 * 32 + b1 * 16
                to_row = (d[2] * 16 + b6 * 8 + b1 * 4 + d[3] * 2) * 8
                pltpu.make_async_remote_copy(
                    src_ref=passing.at[pl.ds(from_row, 16), :],
                    dst_ref=r_ref.at[0, pl.ds(to_row, 16), :],
                    send_sem=pass_send,
                    recv_sem=recv.at[0],
                    device_id=device(xs[dx], ys[0], zs[0]),
                    device_id_type=MESH,
                ).start()
    lax.fori_loop(0, 8, one_away, 0)
    fill_early(d, own, slow, tab)
    fill_middle(d, own, slow, tab4, tab5)
    fill_late(own, slow, tab6, tab7, last)

    def arrive(g):
        pltpu.make_async_copy(r_ref.at[g], r_ref.at[g], recv.at[g]).wait()

    def received(g, c, q):
        return r_ref[g, pl.ds(c * 4 + q, 32, stride=8), :]

    def near(g, c, q):
        return take[c, q] if g == 0 else received(g, c, q)

    arrive(0)
    for q in range(4):
        zero, one = received(0, 0, q), received(0, 1, q)
        take[core, q] = jnp.where(first_core, zero, one)
        give[q] = jnp.where(first_core, one, zero)
    trade = pltpu.make_async_remote_copy(
        src_ref=give,
        dst_ref=take.at[core],
        send_sem=give_send,
        recv_sem=give_recv,
        device_id=sibling,
        device_id_type=MESH,
    )
    trade.start()
    trade.wait()
    arrive(1)
    levels = (state, tab, even_ref, odd_ref)
    early_levels([0, 1], near, *levels)
    arrive(2)
    early_levels([2], received, *levels)
    level_four(1, 2, state, mid, tab4, even4_ref, odd_ref)
    arrive(3)
    early_levels([3], received, *levels)
    level_four(0, 3, state, mid, tab4, even4_ref, odd_ref)
    late_levels(mid, deep, tab5, tab6, tab7, last, fin, even_ref, odd_ref, odd5_ref, o_ref)
    sent = packed.at[pl.ds(0, 992), :]
    pltpu.make_async_copy(sent, sent, send).wait()
    pltpu.make_async_copy(passing, passing, pass_send).wait()


def butterfly(weights, slowness_terms):
    hbm = pl.BlockSpec(memory_space=pltpu.HBM)
    f32, bf16 = jnp.float32, jnp.bfloat16
    return pl.pallas_call(
        kernel,
        out_shape=pltpu.VMEM((2, 256, 256), f32),
        in_specs=[hbm] * 4,
        out_specs=pl.BlockSpec(memory_space=pltpu.VMEM),
        scratch_shapes=[
            pltpu.VMEM((2, 256, 256), f32),
            pltpu.VMEM((2, 128, 256), f32),
            pltpu.VMEM((1024, LANES), f32),
            pltpu.VMEM((1024, LANES), f32),
            pltpu.VMEM((192, LANES), f32),
            pltpu.VMEM((4, 256, LANES), f32),
            pltpu.VMEM((4, 32, LANES), f32),
            pltpu.VMEM((2, 4, 32, LANES), f32),
            pltpu.VMEM((512, 256), f32),
            pltpu.VMEM((256, LANES), f32),
            pltpu.VMEM((1024, 256), bf16),
            pltpu.VMEM((256, 256), bf16),
            pltpu.VMEM((1024, 256), bf16),
            pltpu.VMEM((256, 256), bf16),
            pltpu.SMEM((3,), f32),
            pltpu.VMEM((4, 2, 2, 64, LANES), f32),
            pltpu.VMEM((2, 2, 2, 2, 64, LANES), f32),
            pltpu.VMEM((4, 2, 2, 64, LANES), f32),
            pltpu.VMEM((4, 2, 2, 2, 2, 2, 32, LANES), f32),
            pltpu.VMEM((2, 2, 2, 2, 64, LANES), f32),
            pltpu.VMEM((2, 2, 2, 1, 2, 64, LANES), f32),
            pltpu.VMEM((4, 2, 2, 2, 2, 32, LANES), f32),
            pltpu.VMEM((4, 2, 2, 1, 2, 32, LANES), f32),
            pltpu.VMEM((4, 2, 2, 2, 32, LANES), f32),
            pltpu.VMEM((2, 2, 256, LANES), f32),
            pltpu.SemaphoreType.DMA,
            pltpu.SemaphoreType.DMA,
            pltpu.SemaphoreType.DMA,
            pltpu.SemaphoreType.DMA((3,)),
            pltpu.SemaphoreType.REGULAR,
            pltpu.SemaphoreType.DMA,
            pltpu.SemaphoreType.DMA,
            pltpu.SemaphoreType.DMA,
            pltpu.SemaphoreType.DMA((4,)),
            pltpu.SemaphoreType.DMA,
            pltpu.SemaphoreType.DMA,
        ],
        compiler_params=pltpu.CompilerParams(
            collective_id=0, has_side_effects=True, vmem_limit_bytes=48 * 2**20
        ),
    )(
        *(
            pltpu.with_memory_space_constraint(a, pltpu.HBM)
            for a in (
                weights,
                slowness_terms,
                jnp.asarray(even_matrix()),
                jnp.asarray(odd_matrix()),
            )
        )
    )


def local(weights, slowness_terms):
    return butterfly(weights.reshape(2, 256, 256), slowness_terms).reshape(weights.shape)


def solution(mesh):
    return jax.shard_map(
        local,
        mesh=mesh,
        in_specs=(P(None, "src", "tgt", None, None), P()),
        out_specs=P(None, "src", "tgt", None, None),
        check_vma=False,
    )
```
